32 devices in a mesh: parts: 2 (over x), depth: 8 (over z, y), tile: 2 (over core).
Axes of the slice: x: 2, y: 2, z: 4, core: 2. Of those that a mesh axis runs over, the one named last changes fastest.
Arguments:
- volume: bfloat16 [4, 256, 32, 4096], P(None, ('parts', 'depth'), 'tile'), parts along dimension 1, may hold values from -6 to 6
- brick_mask: int32 [16, 32], P(('parts', 'depth')), parts along dimension 0, may hold values 0 or 1
- brick_order: int32 [16], P('parts'), parts along dimension 0, may hold values from 0 to 7, each once
Outputs:
- picture: float32 [4, 64, 4096], P(None, 'parts', 'depth'), parts along dimension 1
The draws below stay inside these ranges and needn't reach their ends.
There are 2 independent parts, one for each index of `parts`. The reference program is written for one: setup_inputs(seed, part) draws one part's arguments, and reference() takes and returns one part's arrays. A program takes and returns all parts, laid end to end along the dimension named above; each array names one. Nothing has to cross between parts.
Inputs may be any that keep to these rules, and one draw needn't show every extreme that they name: `brick_order`: each slab appears once; position 0 is the front.
All inputs are finite; a program needn't handle non-finite values. No bound on the sum of `brick_mask` on one device may be relied on, other than what follows from the above.
Results may differ from the reference program's by a relative error of at most 0.0003.
Values may be sent and summed in bfloat16 or wider, within the bound.
No kernel may reach another device: no remote copies, remote signals or barrier semaphores. Data moves between devices by JAX's collectives and lax.ppermute only.
A program may use at most 64 MiB of HBM per device.

```python
import jax
import jax.numpy as jnp
from jax import lax

CH = 4
NY = 4096
NZ = 128
NX = 32
SLABS = 8
BLOCKS = 32


def touch_ends(drawn, key, smallest, top_value):
    longest = drawn.shape.index(max(drawn.shape))
    spots = []
    for shift in (0, 1):
        where = [jax.random.randint(jax.random.fold_in(key, axis), (), 0, length) for axis, length in enumerate(drawn.shape)]
        where[longest] = (where[longest] + shift) % drawn.shape[longest]
        spots.append(tuple(where))
    return drawn.at[spots[0]].set(smallest).at[spots[1]].set(top_value)


def block_scale(stream_key, dims, shards, least, top_value):
    factor_of, own = 1.0, jax.random.fold_in(stream_key, 6)
    for position, parts in shards:
        draws = jnp.exp(jax.random.uniform(jax.random.fold_in(own, position), (parts,), jnp.float32, least / len(shards), top_value / len(shards)))
        factor_of = factor_of * jnp.repeat(draws, dims[position] // parts).reshape([-1 if axis == position else 1 for axis in range(len(dims))])
    return factor_of


def scatter_about(rng, dims, scale, reach, split=(), kind=jnp.bfloat16):
    gain = block_scale(rng, dims, split, -0.22, 0.18) if split else 1.0
    array = jax.random.normal(rng, dims, jnp.float32) * scale * gain
    return jnp.minimum(jnp.maximum(array, -reach), reach).astype(kind)


def setup_inputs(seed: int = 0, part: int = 0) -> dict:
    seeds = jax.random.split(jax.random.key(seed), 4)
    own_keys = jax.random.split(jax.random.fold_in(seeds[3], part), 4)
    return {
        "volume": scatter_about(own_keys[0], (CH, NZ, NX, NY), 1.0, 6.0, ((1, 8), (2, 2))),
        "brick_mask": touch_ends((jax.random.randint(own_keys[1], (SLABS, BLOCKS), 0, 2) < 1).astype(jnp.int32), jax.random.fold_in(own_keys[1], 1), 0, 1),
        "brick_order": jax.random.permutation(own_keys[2], SLABS).astype(jnp.int32),
    }


def march(padded, emission, step_size):
    density = padded[1:-1, 1:-1, 1:-1]
    grad_depth = 0.5 * (padded[2:, 1:-1, 1:-1] - padded[:-2, 1:-1, 1:-1])
    grad_rows = 0.5 * (padded[1:-1, 2:, 1:-1] - padded[1:-1, :-2, 1:-1])
    grad_cols = 0.5 * (padded[1:-1, 1:-1, 2:] - padded[1:-1, 1:-1, :-2])
    inverse = lax.rsqrt(1.0 + grad_depth * grad_depth + grad_rows * grad_rows + grad_cols * grad_cols)
    shading = 0.3 + 0.7 * jnp.abs(0.8 * grad_depth + 0.36 * grad_rows + 0.48 * grad_cols) * inverse
    extinction = density * density * step_size
    through = jnp.cumsum(extinction, axis=0)
    before = through - extinction
    weights = (jnp.exp(-before) - jnp.exp(-through)) * shading
    emitted = jax.nn.sigmoid(emission.astype(jnp.float32))
    colour = lax.optimization_barrier(jnp.sum(weights[None] * emitted, axis=1))
    return (colour, through[-1])

def reference(volume, brick_mask, brick_order):
    channels, depth_total, rows_total, cols_total = volume.shape
    slabs = brick_mask.shape[0]
    blocks = brick_mask.shape[1]
    slab_cells = depth_total // slabs
    step_size = 3.0 / depth_total
    keep_cols = jnp.repeat(brick_mask, cols_total // blocks, axis=1).astype(jnp.bfloat16)
    keep_cells = jnp.repeat(keep_cols, slab_cells, axis=0)
    density = volume[0] * keep_cells[:, None, :]
    padded = jnp.pad(density.astype(jnp.float32), 1)
    emission_all = volume[1:]

    def one_slab(slab_index):
        offset = slab_index * slab_cells
        segment = lax.dynamic_slice_in_dim(padded, offset, slab_cells + 2, 0)
        emission = lax.dynamic_slice_in_dim(emission_all, offset, slab_cells, 1)
        return march(segment, emission, step_size)
    colours, optical = lax.map(one_slab, jnp.arange(slabs, dtype=jnp.int32))
    positions = jnp.arange(slabs, dtype=jnp.int32)
    ranking = lax.optimization_barrier(jnp.sum(jnp.where(brick_order[:, None] == positions[None, :], positions[:, None], 0), axis=0))
    in_front = (ranking[None, :] < ranking[:, None]).astype(jnp.float32)
    covered = jnp.einsum('de,exy->dxy', in_front, optical, precision=lax.Precision.HIGHEST)
    blended = lax.optimization_barrier(jnp.sum(jnp.exp(-covered)[:, None] * colours, axis=0))
    opacity = 1.0 - jnp.exp(-lax.optimization_barrier(jnp.sum(optical, axis=0)))
    return jnp.concatenate([blended, opacity[None]], axis=0)
```

```python
import functools
import math

import jax
import jax.numpy as jnp
from jax import lax
from jax.experimental import pallas as pl
from jax.experimental.pallas import tpu as pltpu
from jax.sharding import PartitionSpec as P

LANES = 128


def partners(n, k):
    if n & (n - 1) == 0:
        return [(i, i ^ k) for i in range(n)]
    return [(i, (i + k) % n) for i in range(n)]


def target(n, me, k):
    if n & (n - 1) == 0:
        return lax.bitwise_xor(me, k)
    return lax.rem(me + k, n)


def source(n, me, k):
    if n & (n - 1) == 0:
        return lax.bitwise_xor(me, k)
    return lax.rem(me + n - k, n)


def march_kernel(
    step_size, bricks, strips_ref, mask_ref, side_ref, vol, left, right, low, high, rows_halo, out
):
    depth, rows = vol.shape[1], vol.shape[2]
    strip = strips_ref[pl.program_id(0)]
    lane = lax.broadcasted_iota(jnp.int32, (rows, LANES), 1)
    row = lax.broadcasted_iota(jnp.int32, (rows, LANES), 0)
    first_row, last_row = row == 0, row == rows - 1
    first_lane, last_lane = lane == 0, lane == LANES - 1
    right_half = lane >= LANES // 2
    rate = -step_size * math.log2(math.e)
    to_top = side_ref[0].astype(jnp.float32)
    to_bottom = side_ref[1].astype(jnp.float32)

    for brick in range(bricks):
        cols = pl.ds(brick * LANES, LANES)
        place = strip * bricks + brick + 1
        keep = mask_ref[place] != 0

        @pl.when(jnp.logical_not(keep))
        def _():
            out[0, :, :, cols] = jnp.zeros((4, rows, LANES), jnp.float32)

        @pl.when(keep)
        def _():
            keep_left = mask_ref[place - 1].astype(jnp.float32)
            keep_right = mask_ref[place + 1].astype(jnp.float32)
            keep_side = jnp.where(right_half, keep_left, keep_right)
            halo = rows_halo[:, cols].astype(jnp.float32)
            top, bottom = halo * to_top, halo * to_bottom
            before = low[:, cols].astype(jnp.float32)
            here = vol[0, 0, :, cols].astype(jnp.float32)
            total = jnp.zeros((rows, LANES), jnp.float32)
            clear = jnp.ones((rows, LANES), jnp.float32)
            plain = jnp.zeros((rows, LANES), jnp.float32)
            sums = [jnp.zeros((rows, LANES), jnp.float32) for _ in range(3)]
            for d in range(depth):
                after = (vol[0, d + 1, :, cols] if d + 1 < depth else high[:, cols]).astype(
                    jnp.float32
                )
                prev = vol[0, d, :, pl.ds((brick - 1) * LANES, LANES)] if brick else left[0, d]
                nxt = (
                    vol[0, d, :, pl.ds((brick + 1) * LANES, LANES)]
                    if brick + 1 < bricks
                    else right[0, d]
                )
                side = jnp.where(
                    right_half, prev.astype(jnp.float32), nxt.astype(jnp.float32)
                ) * keep_side
                less = pltpu.roll(jnp.where(last_lane, side, here), 1, 1)
                more = pltpu.roll(jnp.where(first_lane, side, here), LANES - 1, 1)
                up = jnp.where(first_row, top[d : d + 1], pltpu.roll(here, 1, 0))
                down = jnp.where(last_row, bottom[d : d + 1], pltpu.roll(here, rows - 1, 0))
                g_depth, g_rows, g_cols = after - before, down - up, more - less
                square = g_depth * g_depth + g_rows * g_rows + g_cols * g_cols
                toward = jnp.abs(0.28 * g_depth + 0.126 * g_rows + 0.168 * g_cols)
                shading = 0.3 + toward * lax.rsqrt(1.0 + 0.25 * square)
                total = total + here * here
                left_over = jnp.exp2(total * rate)
                weight = (clear - left_over) * shading
                clear = left_over
                plain = plain + weight
                for k in range(3):
                    emission = vol[1 + k, d, :, cols].astype(jnp.float32)
                    sums[k] = sums[k] + weight * jnp.tanh(0.5 * emission)
                before, here = here, after
            for k in range(3):
                out[0, k, :, cols] = 0.5 * (plain + sums[k])
            out[0, 3, :, cols] = total * step_size


def march(volume, low, high, rows_halo, strips, mask, side, step_size, n):
    channels, depth, rows, cols = volume.shape
    strip = cols // n
    bricks = strip // LANES
    blocks = cols // LANES
    spec = pltpu.PrefetchScalarGridSpec(
        num_scalar_prefetch=3,
        grid=(n,),
        in_specs=[
            pl.BlockSpec((channels, depth, rows, strip), lambda j, s, m, t: (0, 0, 0, s[j])),
            pl.BlockSpec(
                (1, depth, rows, LANES),
                lambda j, s, m, t: (0, 0, 0, jnp.maximum(s[j] * bricks - 1, 0)),
            ),
            pl.BlockSpec(
                (1, depth, rows, LANES),
                lambda j, s, m, t: (0, 0, 0, jnp.minimum((s[j] + 1) * bricks, blocks - 1)),
            ),
            pl.BlockSpec((rows, strip), lambda j, s, m, t: (0, s[j])),
            pl.BlockSpec((rows, strip), lambda j, s, m, t: (0, s[j])),
            pl.BlockSpec((depth, strip), lambda j, s, m, t: (0, s[j])),
        ],
        out_specs=pl.BlockSpec((1, 4, rows, strip), lambda j, s, m, t: (j, 0, 0, 0)),
    )
    cells = depth * rows * cols
    return pl.pallas_call(
        functools.partial(march_kernel, step_size, bricks),
        grid_spec=spec,
        out_shape=jax.ShapeDtypeStruct((n, 4, rows, strip), jnp.float32),
        cost_estimate=pl.CostEstimate(
            flops=40 * cells, bytes_accessed=8 * cells, transcendentals=5 * cells
        ),
        compiler_params=pltpu.CompilerParams(
            dimension_semantics=("arbitrary",), vmem_limit_bytes=32 * 1024 * 1024
        ),
        name="march",
    )(strips, mask, side, volume, volume, volume, low, high, rows_halo)


def composite_kernel(n, rank_ref, *refs):
    parts, out = refs[:n], refs[n]
    optical = [part[3] for part in parts]
    whole = optical[0]
    for k in range(1, n):
        whole = whole + optical[k]
    for k in range(n):
        covered = jnp.zeros_like(whole)
        for e in range(n):
            if e != k:
                covered = covered + jnp.where(rank_ref[e] < rank_ref[k], 1.0, 0.0) * optical[e]
        through = jnp.exp(-covered)
        for c in range(3):
            term = through * parts[k][c]
            out[c] = term if k == 0 else out[c] + term
    out[3] = 1.0 - jnp.exp(-whole)


def composite(ranks, parts):
    n = len(parts)
    shape = parts[0].shape
    return pl.pallas_call(
        functools.partial(composite_kernel, n),
        grid_spec=pltpu.PrefetchScalarGridSpec(
            num_scalar_prefetch=1,
            grid=(1,),
            in_specs=[pl.BlockSpec(shape, lambda i, r: (0, 0, 0)) for _ in parts],
            out_specs=pl.BlockSpec(shape, lambda i, r: (0, 0, 0)),
        ),
        out_shape=jax.ShapeDtypeStruct(shape, jnp.float32),
        name="composite",
    )(ranks, *parts)


def on_device(volume, brick_mask, brick_order):
    channels, depth, rows, cols = volume.shape
    n = lax.axis_size("depth")
    tiles = lax.axis_size("tile")
    blocks = brick_mask.shape[1]
    step_size = 3.0 / (depth * n)
    me, tile = lax.axis_index("depth"), lax.axis_index("tile")
    keep = jnp.repeat(brick_mask[0], cols // blocks).astype(jnp.bfloat16)
    mask = jnp.pad(jnp.repeat(brick_mask[0], cols // blocks // LANES), 1)

    up = [(i, i + 1) for i in range(n - 1)]
    down = [(i + 1, i) for i in range(n - 1)]
    assert tiles == 2
    edge = jnp.where(tile == 0, volume[0, :, rows - 1], volume[0, :, 0]) * keep
    rows_halo = lax.ppermute(edge, "tile", [(0, 1), (1, 0)])
    side = jnp.stack([tile, 1 - tile]).astype(jnp.int32)
    low = lax.ppermute(volume[0, depth - 1] * keep, "depth", up)
    high = lax.ppermute(volume[0, 0] * keep, "depth", down)

    strips = jnp.stack([target(n, me, k) for k in range(n)]).astype(jnp.int32)
    bricks = march(volume, low, high, rows_halo, strips, mask, side, step_size, n)
    parts = [bricks[0]]
    for k in range(1, n):
        parts.append(lax.ppermute(bricks[k], "depth", partners(n, k)))
    ranking = jnp.sum(
        jnp.where(
            brick_order[:, None] == jnp.arange(n, dtype=jnp.int32)[None, :],
            jnp.arange(n, dtype=jnp.int32)[:, None],
            0,
        ),
        axis=0,
    )
    sources = jnp.stack([source(n, me, k) for k in range(n)])
    picture = composite(ranking[sources].astype(jnp.int32), parts)
    return lax.all_gather(picture, "tile", axis=1, tiled=True)


def solution(mesh):
    return jax.shard_map(
        on_device,
        mesh=mesh,
        in_specs=(
            P(None, ("parts", "depth"), "tile", None),
            P(("parts", "depth"), None),
            P("parts"),
        ),
        out_specs=P(None, "parts", "depth"),
        check_vma=False,
    )
```

```python
import functools
import math

import jax
import jax.numpy as jnp
from jax import lax
from jax.experimental import pallas as pl
from jax.experimental.pallas import tpu as pltpu
from jax.sharding import PartitionSpec as P

LANES = 128
TOP = 65535.0
HALF = 32768
LARGEST = 36.0
TAU_STEPS = 32000.0

VMEM = pl.BlockSpec(memory_space=pltpu.VMEM)
SMEM = pl.BlockSpec(memory_space=pltpu.SMEM)
HBM = pl.BlockSpec(memory_space=pltpu.HBM)


def rounds(n):
    return list(range(n - 1, -1, -1))


def partners(n, k):
    if n & (n - 1) == 0:
        return [(i, i ^ k) for i in range(n)]
    return [(i, (i + k) % n) for i in range(n)]


def target(n, me, k):
    if n & (n - 1) == 0:
        return lax.bitwise_xor(me, k)
    return lax.rem(me + k, n)


def source(n, me, k):
    if n & (n - 1) == 0:
        return lax.bitwise_xor(me, k)
    return lax.rem(me + n - k, n)


def mask_at(mask, place, blocks):
    inside = jnp.logical_and(place >= 0, place < blocks)
    kept = mask[0, jnp.clip(place, 0, blocks - 1)]
    return jnp.where(inside, kept, 0)


def columns(place):
    return pl.ds(pl.multiple_of(place * LANES, LANES), LANES)


def edges_kernel(mask_hbm, vol, density, first, last, edge, mask, sem, mask_sem):
    depth, rows, cols = density.shape
    copy = pltpu.make_async_copy(vol.at[0], density, sem)
    copy.start()
    mask_copy = pltpu.make_async_copy(mask_hbm, mask, mask_sem)
    mask_copy.start()
    tile = lax.axis_index("tile")
    row = jnp.where(tile == 0, rows - 1, 0)
    at = lax.broadcasted_iota(jnp.int32, (depth, depth * rows), 1)
    cell = lax.broadcasted_iota(jnp.int32, (depth, depth * rows), 0)
    pick = (at == cell * rows + row).astype(jnp.bfloat16)
    mask_copy.wait()
    copy.wait()
    for b in range(cols // LANES):
        keep = mask[0, b].astype(jnp.float32)
        here = pl.ds(b * LANES, LANES)
        planes = density[:, :, here].reshape(depth * rows, LANES)
        border = jnp.dot(pick, planes, preferred_element_type=jnp.float32)
        edge[:, here] = (border * keep).astype(jnp.bfloat16)
        first[:, here] = (density[0, :, here].astype(jnp.float32) * keep).astype(jnp.bfloat16)
        last[:, here] = (density[depth - 1, :, here].astype(jnp.float32) * keep).astype(
            jnp.bfloat16
        )


def edges(volume, mask):
    channels, depth, rows, cols = volume.shape
    plane = jax.ShapeDtypeStruct((rows, cols), jnp.bfloat16)
    return pl.pallas_call(
        edges_kernel,
        in_specs=[HBM, HBM],
        out_specs=[VMEM] * 4,
        out_shape=[
            jax.ShapeDtypeStruct((depth, rows, cols), jnp.bfloat16),
            plane,
            plane,
            jax.ShapeDtypeStruct((depth, cols), jnp.bfloat16),
        ],
        scratch_shapes=[
            pltpu.SMEM(mask.shape, jnp.int32),
            pltpu.SemaphoreType.DMA,
            pltpu.SemaphoreType.DMA,
        ],
        compiler_params=pltpu.CompilerParams(vmem_limit_bytes=48 * 1024 * 1024),
        cost_estimate=pl.CostEstimate(
            flops=1000000, bytes_accessed=2 * depth * rows * cols, transcendentals=0
        ),
        name="edges",
    )(mask, volume)


def march_kernel(step_size, n, mask, vol, density, border, sums_out, ends):
    depth, rows, cols = density.shape
    blocks = cols // LANES
    bricks = blocks // n
    strip = cols // n
    me, tile = lax.axis_index("depth"), lax.axis_index("tile")
    order = rounds(n)

    lane = lax.broadcasted_iota(jnp.int32, (rows, LANES), 1)
    row = lax.broadcasted_iota(jnp.int32, (rows, LANES), 0)
    first_row, last_row = row == 0, row == rows - 1
    first_lane, last_lane = lane == 0, lane == LANES - 1
    right_half = lane >= LANES // 2
    rate = -step_size * math.log2(math.e)
    to_top = tile.astype(jnp.float32)
    to_bottom = 1.0 - to_top

    def one_brick(place):
        here_at = columns(place)
        left_at = columns(jnp.maximum(place - 1, 0))
        right_at = columns(jnp.minimum(place + 1, blocks - 1))
        keep_left = mask_at(mask, place - 1, blocks).astype(jnp.float32)
        keep_right = mask_at(mask, place + 1, blocks).astype(jnp.float32)
        keep_side = jnp.where(right_half, keep_left, keep_right)
        halo = border[:, here_at].astype(jnp.float32)
        top, bottom = halo * to_top, halo * to_bottom
        zeros = jnp.zeros((rows, LANES), jnp.float32)
        total, clear, plain = zeros, jnp.ones((rows, LANES), jnp.float32), zeros
        sums = [zeros for _ in range(3)]
        before = None
        here = density[0, :, here_at].astype(jnp.float32)
        for d in range(depth):
            after = density[d + 1, :, here_at].astype(jnp.float32) if d + 1 < depth else None
            side = (
                jnp.where(
                    right_half,
                    density[d, :, left_at].astype(jnp.float32),
                    density[d, :, right_at].astype(jnp.float32),
                )
                * keep_side
            )
            less = pltpu.roll(jnp.where(last_lane, side, here), 1, 1)
            more = pltpu.roll(jnp.where(first_lane, side, here), LANES - 1, 1)
            up = jnp.where(first_row, top[d : d + 1], pltpu.roll(here, 1, 0))
            down = jnp.where(last_row, bottom[d : d + 1], pltpu.roll(here, rows - 1, 0))
            g_rows, g_cols = down - up, more - less
            flat = g_rows * g_rows + g_cols * g_cols
            slope = 0.126 * g_rows + 0.168 * g_cols
            total = total + here * here
            left_over = jnp.exp2(total * rate)
            weight = clear - left_over
            clear = left_over
            glow = [jnp.tanh(0.5 * vol[1 + k, d, :, here_at].astype(jnp.float32)) for k in range(3)]
            if before is None or after is None:
                end = 0 if before is None else 1
                ends[end, 0, :, here_at] = after if before is None else before
                ends[end, 1, :, here_at] = flat
                ends[end, 2, :, here_at] = slope
                half = 0.5 * weight
                for k in range(3):
                    ends[end, 3 + k, :, here_at] = half + half * glow[k]
            else:
                g_depth = after - before
                shading = 0.3 + jnp.abs(0.28 * g_depth + slope) * lax.rsqrt(
                    1.0 + 0.25 * (g_depth * g_depth + flat)
                )
                weight = weight * shading
                plain = plain + weight
                for k in range(3):
                    sums[k] = sums[k] + weight * glow[k]
            before, here = here, after
        for k in range(3):
            sums_out[k, :, here_at] = 0.5 * (plain + sums[k])
        sums_out[3, :, here_at] = total

    def one_strip(j, carry):
        at = target(n, me, order[0] - j)

        def maybe(b, inner):
            place = at * bricks + b

            @pl.when(mask[0, place] != 0)
            def _():
                one_brick(place)

            return inner

        lax.fori_loop(0, bricks, maybe, 0)
        return carry

    lax.fori_loop(0, n, one_strip, 0)


def march(volume, density, border, mask, step_size, n):
    channels, depth, rows, cols = volume.shape
    cells = depth * rows * cols
    return pl.pallas_call(
        functools.partial(march_kernel, step_size, n),
        in_specs=[SMEM, VMEM, VMEM, VMEM],
        out_specs=[VMEM] * 2,
        out_shape=[
            jax.ShapeDtypeStruct((4, rows, cols), jnp.float32),
            jax.ShapeDtypeStruct((2, 6, rows, cols), jnp.float32),
        ],
        cost_estimate=pl.CostEstimate(
            flops=40 * cells, bytes_accessed=8 * cells, transcendentals=5 * cells
        ),
        compiler_params=pltpu.CompilerParams(vmem_limit_bytes=20 * 1024 * 1024),
        name="march",
    )(mask, volume, density, border)


def finish_kernel(step_size, depth, n, mask, density, sums, ends, low, high, *outs):
    rows, cols = low.shape
    bricks = cols // LANES // n
    me = lax.axis_index("depth")
    scale = TAU_STEPS / (LARGEST * step_size * depth)

    def one_brick(out, place, b):
        here_at, there = columns(place), columns(b)
        colours = [sums[k, :, here_at] for k in range(3)]
        for end, halo in enumerate((low, high)):
            g_depth = ends[end, 0, :, here_at] - halo[:, here_at].astype(jnp.float32)
            if end == 1:
                g_depth = -g_depth
            flat, slope = ends[end, 1, :, here_at], ends[end, 2, :, here_at]
            shading = 0.3 + jnp.abs(0.28 * g_depth + slope) * lax.rsqrt(
                1.0 + 0.25 * (g_depth * g_depth + flat)
            )
            for k in range(3):
                colours[k] = colours[k] + shading * ends[end, 3 + k, :, here_at]
        ticks = sums[3, :, here_at] * (step_size * scale)
        upper = jnp.minimum(ticks.astype(jnp.int32), HALF - 1)
        lower = jnp.minimum((ticks - upper.astype(jnp.float32)) * (2.0 * HALF), TOP)
        lower = lower.astype(jnp.int32)
        optical = (upper.astype(jnp.float32) + lower.astype(jnp.float32) * (0.5 / HALF)) / scale
        opacity = 1.0 - jnp.exp(-optical)
        gain = TOP / jnp.maximum(opacity, 1e-30)
        for k in range(3):
            level = jnp.minimum(colours[k] * gain + 0.5, TOP)
            out[k, :, there] = (level.astype(jnp.int32) - HALF).astype(jnp.int16)
        out[3, :, there] = (upper).astype(jnp.int16)
        out[4, :, there] = (lower - HALF).astype(jnp.int16)

    for j, k in enumerate(rounds(n)):
        at = target(n, me, k)
        out = outs[j]

        def maybe(b, carry, at=at, out=out):
            place = at * bricks + b
            keep = mask[0, place] != 0

            @pl.when(keep)
            def _():
                one_brick(out, place, b)

            @pl.when(jnp.logical_not(keep))
            def _():
                empty = jnp.full((rows, LANES), -HALF, jnp.int32).astype(jnp.int16)
                for c in range(5):
                    out[c, :, columns(b)] = jnp.zeros((rows, LANES), jnp.int16) if c == 3 else empty

            return carry

        lax.fori_loop(0, bricks, maybe, 0)


def finish(density, sums, ends, low, high, mask, step_size, n):
    depth, rows, cols = density.shape
    strip = cols // n
    return pl.pallas_call(
        functools.partial(finish_kernel, step_size, depth, n),
        in_specs=[SMEM] + [VMEM] * 5,
        out_specs=[VMEM] * n,
        out_shape=[jax.ShapeDtypeStruct((5, rows, strip), jnp.int16)] * n,
        cost_estimate=pl.CostEstimate(
            flops=60 * rows * cols, bytes_accessed=64 * rows * cols, transcendentals=4 * rows * cols
        ),
        compiler_params=pltpu.CompilerParams(vmem_limit_bytes=16 * 1024 * 1024),
        name="finish",
    )(mask, density, sums, ends, low, high)


def composite_kernel(step_size, depth, n, order, *refs):
    parts, out, ranks = refs[:n], refs[n], refs[n + 1]
    me = lax.axis_index("depth")
    scale = TAU_STEPS / (LARGEST * step_size * depth)
    for p in range(n):
        ranks[order[p]] = p
    rank = [ranks[source(n, me, k)] for k in rounds(n)]
    rows, strip = out.shape[1:]
    for b in range(strip // LANES):
        at = pl.ds(b * LANES, LANES)
        optical = [
            (
                part[3, :, at].astype(jnp.float32)
                + (part[4, :, at].astype(jnp.float32) + float(HALF)) * (0.5 / HALF)
            )
            / scale
            for part in parts
        ]
        whole = optical[0]
        for k in range(1, n):
            whole = whole + optical[k]
        picture = [None] * 3
        for k in range(n):
            covered = jnp.zeros_like(whole)
            for e in range(n):
                if e != k:
                    covered = covered + jnp.where(rank[e] < rank[k], 1.0, 0.0) * optical[e]
            share = jnp.exp(-covered) * (1.0 - jnp.exp(-optical[k])) * (1.0 / TOP)
            for c in range(3):
                term = share * (parts[k][c, :, at].astype(jnp.float32) + float(HALF))
                picture[c] = term if k == 0 else picture[c] + term
        for c in range(3):
            out[c, :, at] = picture[c]
        out[3, :, at] = 1.0 - jnp.exp(-whole)


def composite(order, parts, step_size, depth):
    n = len(parts)
    rows, strip = parts[0].shape[1:]
    return pl.pallas_call(
        functools.partial(composite_kernel, step_size, depth, n),
        in_specs=[SMEM] + [VMEM] * n,
        out_specs=VMEM,
        out_shape=jax.ShapeDtypeStruct((4, rows, strip), jnp.float32),
        scratch_shapes=[pltpu.SMEM((n,), jnp.int32)],
        compiler_params=pltpu.CompilerParams(vmem_limit_bytes=16 * 1024 * 1024),
        name="composite",
    )(order, *parts)


def on_device(volume, brick_mask, brick_order):
    channels, depth, rows, cols = volume.shape
    n = lax.axis_size("depth")
    assert lax.axis_size("tile") == 2
    step_size = 3.0 / (depth * n)
    mask = jnp.repeat(brick_mask, cols // brick_mask.shape[1] // LANES, axis=1)

    up = [(i, i + 1) for i in range(n - 1)]
    down = [(i + 1, i) for i in range(n - 1)]
    density, first, last, edge = edges(volume, mask)
    border = lax.ppermute(edge, "tile", [(0, 1), (1, 0)])
    low = lax.ppermute(last, "depth", up)
    high = lax.ppermute(first, "depth", down)
    sums, ends = march(volume, density, border, mask, step_size, n)
    strips = finish(density, sums, ends, low, high, mask, step_size, n)
    parts = [
        lax.ppermute(strip, "depth", partners(n, k)) if k else strip
        for strip, k in zip(strips, rounds(n))
    ]
    picture = composite(brick_order, parts, step_size, depth)
    return lax.all_gather(picture, "tile", axis=1, tiled=True)


def solution(mesh):
    return jax.shard_map(
        on_device,
        mesh=mesh,
        in_specs=(
            P(None, ("parts", "depth"), "tile", None),
            P(("parts", "depth"), None),
            P("parts"),
        ),
        out_specs=P(None, "parts", "depth"),
        check_vma=False,
    )
```

```python
import functools
import math

import jax
import jax.numpy as jnp
from jax import lax
from jax.experimental import pallas as pl
from jax.experimental.pallas import tpu as pltpu
from jax.sharding import PartitionSpec as P

LANES = 128
TOP = 65535.0
HALF = 32768
LARGEST = 36.0
TAU_STEPS = 32000.0

VMEM = pl.BlockSpec(memory_space=pltpu.VMEM)
SMEM = pl.BlockSpec(memory_space=pltpu.SMEM)
HBM = pl.BlockSpec(memory_space=pltpu.HBM)


def rounds(n):
    return list(range(n - 1, -1, -1))


def partners(n, k):
    if n & (n - 1) == 0:
        return [(i, i ^ k) for i in range(n)]
    return [(i, (i + k) % n) for i in range(n)]


def target(n, me, k):
    if n & (n - 1) == 0:
        return lax.bitwise_xor(me, k)
    return lax.rem(me + k, n)


def source(n, me, k):
    if n & (n - 1) == 0:
        return lax.bitwise_xor(me, k)
    return lax.rem(me + n - k, n)


def mask_at(mask, place, blocks):
    inside = jnp.logical_and(place >= 0, place < blocks)
    kept = mask[0, jnp.clip(place, 0, blocks - 1)]
    return jnp.where(inside, kept, 0)


def columns(place):
    return pl.ds(pl.multiple_of(place * LANES, LANES), LANES)


def edges_kernel(mask_hbm, vol, density, near, far, edge, mask, sem, mask_sem):
    depth, rows, cols = density.shape
    copy = pltpu.make_async_copy(vol.at[0], density, sem)
    copy.start()
    mask_copy = pltpu.make_async_copy(mask_hbm, mask, mask_sem)
    mask_copy.start()
    row = jnp.where(lax.axis_index("tile") == 0, rows - 1, 0)
    even = lax.rem(lax.axis_index("depth"), 2) == 0
    at = lax.broadcasted_iota(jnp.int32, (depth, depth * rows), 1)
    cell = lax.broadcasted_iota(jnp.int32, (depth, depth * rows), 0)
    pick = (at == cell * rows + row).astype(jnp.bfloat16)
    mask_copy.wait()
    copy.wait()
    for b in range(cols // LANES):
        keep = mask[0, b].astype(jnp.float32)
        here = pl.ds(b * LANES, LANES)
        planes = density[:, :, here].reshape(depth * rows, LANES)
        border = jnp.dot(pick, planes, preferred_element_type=jnp.float32)
        edge[:, here] = (border * keep).astype(jnp.bfloat16)
        first = density[0, :, here].astype(jnp.float32) * keep
        last = density[depth - 1, :, here].astype(jnp.float32) * keep
        near[:, here] = jnp.where(even, last, first).astype(jnp.bfloat16)
        far[:, here] = jnp.where(even, first, last).astype(jnp.bfloat16)


def edges(volume, mask):
    channels, depth, rows, cols = volume.shape
    plane = jax.ShapeDtypeStruct((rows, cols), jnp.bfloat16)
    return pl.pallas_call(
        edges_kernel,
        in_specs=[HBM, HBM],
        out_specs=[VMEM] * 4 + [SMEM],
        out_shape=[
            jax.ShapeDtypeStruct((depth, rows, cols), jnp.bfloat16),
            plane,
            plane,
            jax.ShapeDtypeStruct((depth, cols), jnp.bfloat16),
            jax.ShapeDtypeStruct(mask.shape, jnp.int32),
        ],
        scratch_shapes=[pltpu.SemaphoreType.DMA, pltpu.SemaphoreType.DMA],
        compiler_params=pltpu.CompilerParams(vmem_limit_bytes=48 * 1024 * 1024),
        cost_estimate=pl.CostEstimate(
            flops=1000000, bytes_accessed=2 * depth * rows * cols, transcendentals=0
        ),
        name="edges",
    )(mask, volume)


def shade(g_depth, flat, slope):
    return 0.3 + jnp.abs(0.28 * g_depth + slope) * lax.rsqrt(1.0 + 0.25 * (g_depth * g_depth + flat))


def halves(even, near, far, where):
    near = near[:, where].astype(jnp.float32)
    far = far[:, where].astype(jnp.float32)
    return jnp.where(even, far, near), jnp.where(even, near, far)


def march_brick(step_size, vol, density, border, mask, place, planes, put_end, put):
    depth, rows, cols = density.shape
    blocks = cols // LANES
    lane = lax.broadcasted_iota(jnp.int32, (rows, LANES), 1)
    row = lax.broadcasted_iota(jnp.int32, (rows, LANES), 0)
    first_row, last_row = row == 0, row == rows - 1
    first_lane, last_lane = lane == 0, lane == LANES - 1
    right_half = lane >= LANES // 2
    rate = -step_size * math.log2(math.e)
    to_top = lax.axis_index("tile").astype(jnp.float32)
    here_at = columns(place)
    left_at = columns(jnp.maximum(place - 1, 0))
    right_at = columns(jnp.minimum(place + 1, blocks - 1))
    keep_left = mask_at(mask, place - 1, blocks).astype(jnp.float32)
    keep_right = mask_at(mask, place + 1, blocks).astype(jnp.float32)
    keep_side = jnp.where(right_half, keep_left, keep_right)
    halo = border[:, here_at].astype(jnp.float32)
    top, bottom = halo * to_top, halo * (1.0 - to_top)
    zeros = jnp.zeros((rows, LANES), jnp.float32)
    total, clear, plain = zeros, jnp.ones((rows, LANES), jnp.float32), zeros
    sums = [zeros for _ in range(3)]
    before = planes[0] if planes else None
    here = density[0, :, here_at].astype(jnp.float32)
    for d in range(depth):
        if d + 1 < depth:
            after = density[d + 1, :, here_at].astype(jnp.float32)
        else:
            after = planes[1] if planes else None
        left = density[d, :, left_at].astype(jnp.float32)
        right = density[d, :, right_at].astype(jnp.float32)
        side = jnp.where(right_half, left, right) * keep_side
        less = pltpu.roll(jnp.where(last_lane, side, here), 1, 1)
        more = pltpu.roll(jnp.where(first_lane, side, here), LANES - 1, 1)
        up = jnp.where(first_row, top[d : d + 1], pltpu.roll(here, 1, 0))
        down = jnp.where(last_row, bottom[d : d + 1], pltpu.roll(here, rows - 1, 0))
        g_rows, g_cols = down - up, more - less
        flat = g_rows * g_rows + g_cols * g_cols
        slope = 0.126 * g_rows + 0.168 * g_cols
        total = total + here * here
        left_over = jnp.exp2(total * rate)
        weight = clear - left_over
        clear = left_over
        glow = [jnp.tanh(0.5 * vol[1 + k, d, :, here_at].astype(jnp.float32)) for k in range(3)]
        if before is None or after is None:
            inner = after if before is None else before
            half = 0.5 * weight
            put_end(0 if d == 0 else 1, [inner, flat, slope] + [half + half * g for g in glow])
        else:
            weight = weight * shade(after - before, flat, slope)
            plain = plain + weight
            for k in range(3):
                sums[k] = sums[k] + weight * glow[k]
        before, here = here, after
    put([0.5 * (plain + sums[k]) for k in range(3)], total)


def scale_of(step_size, depth):
    return TAU_STEPS / (LARGEST * step_size * depth)


def encode(out, there, colours, total, step_size, depth):
    scale = scale_of(step_size, depth)
    ticks = total * (step_size * scale)
    upper = jnp.minimum(ticks.astype(jnp.int32), HALF - 1)
    lower = jnp.minimum((ticks - upper.astype(jnp.float32)) * (2.0 * HALF), TOP).astype(jnp.int32)
    optical = (upper.astype(jnp.float32) + lower.astype(jnp.float32) * (0.5 / HALF)) * (1.0 / scale)
    opacity = 1.0 - jnp.exp(-optical)
    gain = TOP / jnp.maximum(opacity, 1e-30)
    for k in range(3):
        level = jnp.minimum(colours[k] * gain + 0.5, TOP)
        out[k, :, there] = (level.astype(jnp.int32) - HALF).astype(jnp.int16)
    out[3, :, there] = upper.astype(jnp.int16)
    out[4, :, there] = (lower - HALF).astype(jnp.int16)


def far_kernel(step_size, n, ks, mask, vol, density, border, sums_out, ends):
    depth, rows, cols = density.shape
    bricks = cols // LANES // n
    me = lax.axis_index("depth")

    def step(i, carry):
        place = target(n, me, ks[0] - i // bricks) * bricks + i % bricks
        here = columns(i)

        def put_end(end, values):
            for v, value in enumerate(values):
                ends[end, v, :, here] = value

        def put(colours, total):
            for v, value in enumerate(colours + [total]):
                sums_out[v, :, here] = value

        keep = mask[0, place] != 0

        @pl.when(keep)
        def _():
            march_brick(
                step_size, vol, density, border, mask, place, None, put_end, put
            )

        @pl.when(jnp.logical_not(keep))
        def _():
            empty = jnp.zeros((rows, LANES), jnp.float32)
            put([empty] * 3, empty)
            put_end(0, [empty] * 6)
            put_end(1, [empty] * 6)

        return carry

    lax.fori_loop(0, len(ks) * bricks, step, 0)


def costs(cells):
    return pl.CostEstimate(flops=40 * cells, bytes_accessed=8 * cells, transcendentals=5 * cells)


def march_far(volume, density, border, mask, step_size, n, ks):
    channels, depth, rows, cols = volume.shape
    width = cols // n * len(ks)
    return pl.pallas_call(
        functools.partial(far_kernel, step_size, n, ks),
        in_specs=[SMEM, VMEM, VMEM, VMEM],
        out_specs=[VMEM] * 2,
        out_shape=[
            jax.ShapeDtypeStruct((4, rows, width), jnp.float32),
            jax.ShapeDtypeStruct((2, 6, rows, width), jnp.float32),
        ],
        cost_estimate=costs(depth * rows * width),
        compiler_params=pltpu.CompilerParams(vmem_limit_bytes=20 * 1024 * 1024),
        name="march_far",
    )(mask, volume, density, border)


def finish_kernel(step_size, depth, n, ks, sums, ends, near, far, *outs):
    rows, cols = near.shape
    strip = cols // n
    width = math.gcd(strip, 2 * LANES)
    me = lax.axis_index("depth")
    even = lax.rem(me, 2) == 0
    for j, k in enumerate(ks):
        at = target(n, me, k) * strip
        for c in range(strip // width):
            here = pl.ds(j * strip + c * width, width)
            planes = halves(
                even, near, far, pl.ds(pl.multiple_of(at + c * width, LANES), width)
            )
            colours = [sums[v, :, here] for v in range(3)]
            for end in range(2):
                g_depth = ends[end, 0, :, here] - planes[end]
                if end == 1:
                    g_depth = -g_depth
                shading = shade(g_depth, ends[end, 1, :, here], ends[end, 2, :, here])
                for v in range(3):
                    colours[v] = colours[v] + shading * ends[end, 3 + v, :, here]
            encode(outs[j], pl.ds(c * width, width), colours, sums[3, :, here], step_size, depth)


def finish(sums, ends, near, far, step_size, depth, n, ks):
    rows, cols = near.shape
    cells = rows * cols // n * len(ks)
    return pl.pallas_call(
        functools.partial(finish_kernel, step_size, depth, n, ks),
        in_specs=[VMEM] * 4,
        out_specs=[VMEM] * len(ks),
        out_shape=[jax.ShapeDtypeStruct((5, rows, cols // n), jnp.int16)] * len(ks),
        cost_estimate=pl.CostEstimate(
            flops=60 * cells, bytes_accessed=64 * cells, transcendentals=4 * cells
        ),
        compiler_params=pltpu.CompilerParams(vmem_limit_bytes=16 * 1024 * 1024),
        name="finish",
    )(sums, ends, near, far)


def near_kernel(step_size, n, ks, mask, vol, density, border, near, far, *outs):
    depth, rows, cols = density.shape
    bricks = cols // LANES // n
    me = lax.axis_index("depth")
    even = lax.rem(me, 2) == 0
    for k, out in zip(ks, outs):
        at = target(n, me, k)

        def step(b, carry, at=at, out=out):
            place = at * bricks + b
            there = columns(b)
            keep = mask[0, place] != 0

            @pl.when(keep)
            def _():
                planes = halves(even, near, far, columns(place))

                def put(colours, total):
                    encode(out, there, colours, total, step_size, depth)

                march_brick(
                    step_size, vol, density, border, mask, place, planes, None, put
                )

            @pl.when(jnp.logical_not(keep))
            def _():
                low = jnp.full((rows, LANES), -HALF, jnp.int32).astype(jnp.int16)
                for c in range(5):
                    out[c, :, there] = jnp.zeros((rows, LANES), jnp.int16) if c == 3 else low

            return carry

        lax.fori_loop(0, bricks, step, 0)


def march_near(volume, density, border, near, far, mask, step_size, n, ks):
    channels, depth, rows, cols = volume.shape
    width = cols // n * len(ks)
    return pl.pallas_call(
        functools.partial(near_kernel, step_size, n, ks),
        in_specs=[SMEM] + [VMEM] * 5,
        out_specs=[VMEM] * len(ks),
        out_shape=[jax.ShapeDtypeStruct((5, rows, cols // n), jnp.int16)] * len(ks),
        cost_estimate=costs(depth * rows * width),
        compiler_params=pltpu.CompilerParams(vmem_limit_bytes=20 * 1024 * 1024),
        name="march_near",
    )(mask, volume, density, border, near, far)


def composite_kernel(step_size, depth, n, order, *refs):
    parts, out, ranks = refs[:n], refs[n], refs[n + 1]
    me = lax.axis_index("depth")
    scale = scale_of(step_size, depth)
    for p in range(n):
        ranks[order[p]] = p
    rank = [ranks[source(n, me, k)] for k in rounds(n)]
    rows, strip = out.shape[1:]
    for b in range(strip // LANES):
        at = pl.ds(b * LANES, LANES)
        optical = [
            (
                part[3, :, at].astype(jnp.float32)
                + (part[4, :, at].astype(jnp.float32) + float(HALF)) * (0.5 / HALF)
            )
            * (1.0 / scale)
            for part in parts
        ]
        whole = optical[0]
        for k in range(1, n):
            whole = whole + optical[k]
        picture = [None] * 3
        for k in range(n):
            covered = jnp.zeros_like(whole)
            for e in range(n):
                if e != k:
                    covered = covered + jnp.where(rank[e] < rank[k], 1.0, 0.0) * optical[e]
            share = jnp.exp(-covered) * (1.0 - jnp.exp(-optical[k])) * (1.0 / TOP)
            for c in range(3):
                term = share * (parts[k][c, :, at].astype(jnp.float32) + float(HALF))
                picture[c] = term if k == 0 else picture[c] + term
        for c in range(3):
            out[c, :, at] = picture[c]
        out[3, :, at] = 1.0 - jnp.exp(-whole)


def composite(order, parts, step_size, depth):
    n = len(parts)
    rows, strip = parts[0].shape[1:]
    return pl.pallas_call(
        functools.partial(composite_kernel, step_size, depth, n),
        in_specs=[SMEM] + [VMEM] * n,
        out_specs=VMEM,
        out_shape=jax.ShapeDtypeStruct((4, rows, strip), jnp.float32),
        scratch_shapes=[pltpu.SMEM((n,), jnp.int32)],
        compiler_params=pltpu.CompilerParams(vmem_limit_bytes=16 * 1024 * 1024),
        name="composite",
    )(order, *parts)


def on_device(volume, brick_mask, brick_order):
    channels, depth, rows, cols = volume.shape
    n = lax.axis_size("depth")
    assert lax.axis_size("tile") == 2
    step_size = 3.0 / (depth * n)
    mask = jnp.repeat(brick_mask, cols // brick_mask.shape[1] // LANES, axis=1)

    density, near, far, edge, mask = edges(volume, mask)
    border = lax.ppermute(edge, "tile", [(0, 1), (1, 0)])
    pairs = [(i, i ^ 1) for i in range(n) if i ^ 1 < n]
    near = lax.ppermute(near, "depth", pairs)
    pairs = [(i, i + 1) for i in range(1, n - 1, 2)]
    far = lax.ppermute(far, "depth", pairs + [(b, a) for a, b in pairs])

    first, second = rounds(n)[: n // 2], rounds(n)[n // 2 :]
    sums, ends = march_far(volume, density, border, mask, step_size, n, first)
    strips = finish(sums, ends, near, far, step_size, depth, n, first)
    strips, mask = lax.optimization_barrier((strips, mask))
    strips = list(strips) + list(
        march_near(volume, density, border, near, far, mask, step_size, n, second)
    )
    parts = [
        lax.ppermute(strip, "depth", partners(n, k)) if k else strip
        for strip, k in zip(strips, rounds(n))
    ]
    picture = composite(brick_order, parts, step_size, depth)
    return lax.all_gather(picture, "tile", axis=1, tiled=True)


def solution(mesh):
    return jax.shard_map(
        on_device,
        mesh=mesh,
        in_specs=(
            P(None, ("parts", "depth"), "tile", None),
            P(("parts", "depth"), None),
            P("parts"),
        ),
        out_specs=P(None, "parts", "depth"),
        check_vma=False,
    )
```

```python
import functools
import math

import jax
import jax.numpy as jnp
from jax import lax
from jax.experimental import pallas as pl
from jax.experimental.pallas import tpu as pltpu
from jax.sharding import PartitionSpec as P

LANES = 128
TOP = 65535.0
HALF = 32768

VMEM = pl.BlockSpec(memory_space=pltpu.VMEM)
SMEM = pl.BlockSpec(memory_space=pltpu.SMEM)
HBM = pl.BlockSpec(memory_space=pltpu.HBM)


def rounds(n):
    return list(range(n - 1, -1, -1))


def partners(n, k):
    if n & (n - 1) == 0:
        return [(i, i ^ k) for i in range(n)]
    return [(i, (i + k) % n) for i in range(n)]


def target(n, me, k):
    if n & (n - 1) == 0:
        return lax.bitwise_xor(me, k)
    return lax.rem(me + k, n)


def source(n, me, k):
    if n & (n - 1) == 0:
        return lax.bitwise_xor(me, k)
    return lax.rem(me + n - k, n)


def mask_at(mask, place, blocks):
    inside = jnp.logical_and(place >= 0, place < blocks)
    kept = mask[0, jnp.clip(place, 0, blocks - 1)]
    return jnp.where(inside, kept, 0)


def columns(place):
    return pl.ds(pl.multiple_of(place * LANES, LANES), LANES)


def edges_kernel(mask_hbm, vol, density, near, far, edge, mask, sem, mask_sem):
    depth, rows, cols = density.shape
    copy = pltpu.make_async_copy(vol.at[0], density, sem)
    copy.start()
    mask_copy = pltpu.make_async_copy(mask_hbm, mask, mask_sem)
    mask_copy.start()
    row = jnp.where(lax.axis_index("tile") == 0, rows - 1, 0)
    even = lax.rem(lax.axis_index("depth"), 2) == 0
    at = lax.broadcasted_iota(jnp.int32, (depth, depth * rows), 1)
    cell = lax.broadcasted_iota(jnp.int32, (depth, depth * rows), 0)
    pick = (at == cell * rows + row).astype(jnp.bfloat16)
    mask_copy.wait()
    copy.wait()
    for b in range(cols // LANES):
        keep = mask[0, b].astype(jnp.float32)
        here = pl.ds(b * LANES, LANES)
        planes = density[:, :, here].reshape(depth * rows, LANES)
        border = jnp.dot(pick, planes, preferred_element_type=jnp.float32)
        edge[:, here] = (border * keep).astype(jnp.bfloat16)
        first = density[0, :, here].astype(jnp.float32) * keep
        last = density[depth - 1, :, here].astype(jnp.float32) * keep
        near[:, here] = jnp.where(even, last, first).astype(jnp.bfloat16)
        far[:, here] = jnp.where(even, first, last).astype(jnp.bfloat16)


def edges(volume, mask):
    channels, depth, rows, cols = volume.shape
    plane = jax.ShapeDtypeStruct((rows, cols), jnp.bfloat16)
    return pl.pallas_call(
        edges_kernel,
        in_specs=[HBM, HBM],
        out_specs=[VMEM] * 4 + [SMEM],
        out_shape=[
            jax.ShapeDtypeStruct((depth, rows, cols), jnp.bfloat16),
            plane,
            plane,
            jax.ShapeDtypeStruct((depth, cols), jnp.bfloat16),
            jax.ShapeDtypeStruct(mask.shape, jnp.int32),
        ],
        scratch_shapes=[pltpu.SemaphoreType.DMA, pltpu.SemaphoreType.DMA],
        compiler_params=pltpu.CompilerParams(vmem_limit_bytes=48 * 1024 * 1024),
        cost_estimate=pl.CostEstimate(
            flops=1000000, bytes_accessed=2 * depth * rows * cols, transcendentals=0
        ),
        name="edges",
    )(mask, volume)


def shade(g_depth, flat, slope):
    return 0.3 + jnp.abs(0.28 * g_depth + slope) * lax.rsqrt(1.0 + 0.25 * (g_depth * g_depth + flat))


def halves(even, near, far, where):
    near = near[:, where].astype(jnp.float32)
    far = far[:, where].astype(jnp.float32)
    return jnp.where(even, far, near), jnp.where(even, near, far)


def march_brick(step_size, vol, density, border, mask, place, planes, put_end, put):
    depth, rows, cols = density.shape
    blocks = cols // LANES
    lane = lax.broadcasted_iota(jnp.int32, (rows, LANES), 1)
    row = lax.broadcasted_iota(jnp.int32, (rows, LANES), 0)
    first_row, last_row = row == 0, row == rows - 1
    first_lane, last_lane = lane == 0, lane == LANES - 1
    right_half = lane >= LANES // 2
    rate = -step_size * math.log2(math.e)
    to_top = lax.axis_index("tile").astype(jnp.float32)
    here_at = columns(place)
    left_at = columns(jnp.maximum(place - 1, 0))
    right_at = columns(jnp.minimum(place + 1, blocks - 1))
    keep_left = mask_at(mask, place - 1, blocks).astype(jnp.float32)
    keep_right = mask_at(mask, place + 1, blocks).astype(jnp.float32)
    keep_side = jnp.where(right_half, keep_left, keep_right)
    halo = border[:, here_at].astype(jnp.float32)
    top, bottom = halo * to_top, halo * (1.0 - to_top)
    zeros = jnp.zeros((rows, LANES), jnp.float32)
    total, clear, plain = zeros, jnp.ones((rows, LANES), jnp.float32), zeros
    sums = [zeros for _ in range(3)]
    before = planes[0] if planes else None
    here = density[0, :, here_at].astype(jnp.float32)
    for d in range(depth):
        if d + 1 < depth:
            after = density[d + 1, :, here_at].astype(jnp.float32)
        else:
            after = planes[1] if planes else None
        left = density[d, :, left_at].astype(jnp.float32)
        right = density[d, :, right_at].astype(jnp.float32)
        side = jnp.where(right_half, left, right) * keep_side
        less = pltpu.roll(jnp.where(last_lane, side, here), 1, 1)
        more = pltpu.roll(jnp.where(first_lane, side, here), LANES - 1, 1)
        up = jnp.where(first_row, top[d : d + 1], pltpu.roll(here, 1, 0))
        down = jnp.where(last_row, bottom[d : d + 1], pltpu.roll(here, rows - 1, 0))
        g_rows, g_cols = down - up, more - less
        flat = g_rows * g_rows + g_cols * g_cols
        slope = 0.126 * g_rows + 0.168 * g_cols
        total = total + here * here
        left_over = jnp.exp2(total * rate)
        weight = clear - left_over
        clear = left_over
        glow = [jnp.tanh(0.5 * vol[1 + k, d, :, here_at].astype(jnp.float32)) for k in range(3)]
        if before is None or after is None:
            inner = after if before is None else before
            half = 0.5 * weight
            put_end(0 if d == 0 else 1, [inner, flat, slope] + [half + half * g for g in glow])
        else:
            weight = weight * shade(after - before, flat, slope)
            plain = plain + weight
            for k in range(3):
                sums[k] = sums[k] + weight * glow[k]
        before, here = here, after
    put([0.5 * (plain + sums[k]) for k in range(3)], clear)


def encode(out, there, colours, clear):
    root = jnp.sqrt(jnp.sqrt(jnp.sqrt(1.0 - clear)))
    level = (root * TOP + 0.5).astype(jnp.int32)
    out[3, :, there] = (level - HALF).astype(jnp.int16)
    gain = TOP / jnp.maximum(eighth_power(level.astype(jnp.float32) * (1.0 / TOP)), 1e-30)
    for k in range(3):
        level = jnp.minimum(colours[k] * gain + 0.5, TOP)
        out[k, :, there] = (level.astype(jnp.int32) - HALF).astype(jnp.int16)


def eighth_power(root):
    square = root * root
    square = square * square
    return square * square


def far_kernel(step_size, n, ks, mask, vol, density, border, sums_out, ends):
    depth, rows, cols = density.shape
    bricks = cols // LANES // n
    me = lax.axis_index("depth")

    def step(i, carry):
        place = target(n, me, lax.select(i // bricks < n // 2, n - 1 - i // bricks, 0)) * bricks + i % bricks
        here = columns(i)

        def put_end(end, values):
            for v, value in enumerate(values):
                ends[end, v, :, here] = value

        def put(colours, clear):
            for v, value in enumerate(colours + [clear]):
                sums_out[v, :, here] = value

        keep = mask[0, place] != 0

        @pl.when(keep)
        def _():
            march_brick(
                step_size, vol, density, border, mask, place, None, put_end, put
            )

        @pl.when(jnp.logical_not(keep))
        def _():
            empty = jnp.zeros((rows, LANES), jnp.float32)
            put([empty] * 3, empty + 1.0)
            put_end(0, [empty] * 6)
            put_end(1, [empty] * 6)

        return carry

    lax.fori_loop(0, len(ks) * bricks, step, 0)


def costs(cells):
    return pl.CostEstimate(flops=40 * cells, bytes_accessed=8 * cells, transcendentals=5 * cells)


def march_far(volume, density, border, mask, step_size, n, ks):
    channels, depth, rows, cols = volume.shape
    width = cols // n * len(ks)
    return pl.pallas_call(
        functools.partial(far_kernel, step_size, n, ks),
        in_specs=[SMEM, VMEM, VMEM, VMEM],
        out_specs=[VMEM] * 2,
        out_shape=[
            jax.ShapeDtypeStruct((4, rows, width), jnp.float32),
            jax.ShapeDtypeStruct((2, 6, rows, width), jnp.float32),
        ],
        cost_estimate=costs(depth * rows * width),
        compiler_params=pltpu.CompilerParams(vmem_limit_bytes=20 * 1024 * 1024),
        name="march_far",
    )(mask, volume, density, border)


def finish_kernel(n, ks, sums, ends, near, far, *outs):
    rows, cols = near.shape
    strip = cols // n
    width = math.gcd(strip, 2 * LANES)
    me = lax.axis_index("depth")
    even = lax.rem(me, 2) == 0
    for j, k in enumerate(ks):
        at = target(n, me, k) * strip
        for c in range(strip // width):
            here = pl.ds(j * strip + c * width, width)
            planes = halves(
                even, near, far, pl.ds(pl.multiple_of(at + c * width, LANES), width)
            )
            colours = [sums[v, :, here] for v in range(3)]
            for end in range(2):
                g_depth = ends[end, 0, :, here] - planes[end]
                if end == 1:
                    g_depth = -g_depth
                shading = shade(g_depth, ends[end, 1, :, here], ends[end, 2, :, here])
                for v in range(3):
                    colours[v] = colours[v] + shading * ends[end, 3 + v, :, here]
            encode(outs[j], pl.ds(c * width, width), colours, sums[3, :, here])


def finish(sums, ends, near, far, n, ks):
    rows, cols = near.shape
    cells = rows * cols // n * len(ks)
    return pl.pallas_call(
        functools.partial(finish_kernel, n, ks),
        in_specs=[VMEM] * 4,
        out_specs=[VMEM] * len(ks),
        out_shape=[jax.ShapeDtypeStruct((4, rows, cols // n), jnp.int16)] * len(ks),
        cost_estimate=pl.CostEstimate(
            flops=60 * cells, bytes_accessed=64 * cells, transcendentals=4 * cells
        ),
        compiler_params=pltpu.CompilerParams(vmem_limit_bytes=16 * 1024 * 1024),
        name="finish",
    )(sums, ends, near, far)


def near_kernel(step_size, n, ks, mask, vol, density, border, near, far, *outs):
    depth, rows, cols = density.shape
    bricks = cols // LANES // n
    me = lax.axis_index("depth")
    even = lax.rem(me, 2) == 0
    for k, out in zip(ks, outs):
        at = target(n, me, k)

        def step(b, carry, at=at, out=out):
            place = at * bricks + b
            there = columns(b)
            keep = mask[0, place] != 0

            @pl.when(keep)
            def _():
                planes = halves(even, near, far, columns(place))

                def put(colours, clear):
                    encode(out, there, colours, clear)

                march_brick(
                    step_size, vol, density, border, mask, place, planes, None, put
                )

            @pl.when(jnp.logical_not(keep))
            def _():
                low = jnp.full((rows, LANES), -HALF, jnp.int32).astype(jnp.int16)
                for c in range(4):
                    out[c, :, there] = low

            return carry

        lax.fori_loop(0, bricks, step, 0)


def march_near(volume, density, border, near, far, mask, step_size, n, ks):
    channels, depth, rows, cols = volume.shape
    width = cols // n * len(ks)
    return pl.pallas_call(
        functools.partial(near_kernel, step_size, n, ks),
        in_specs=[SMEM] + [VMEM] * 5,
        out_specs=[VMEM] * len(ks),
        out_shape=[jax.ShapeDtypeStruct((4, rows, cols // n), jnp.int16)] * len(ks),
        cost_estimate=costs(depth * rows * width),
        compiler_params=pltpu.CompilerParams(vmem_limit_bytes=20 * 1024 * 1024),
        name="march_near",
    )(mask, volume, density, border, near, far)


def composite_kernel(ks, order, *refs):
    n = len(ks)
    parts, out, ranks = refs[:n], refs[n], refs[n + 1]
    me = lax.axis_index("depth")
    for p in range(n):
        ranks[order[p]] = p
    rank = [ranks[source(n, me, k)] for k in ks]
    before = [[jnp.where(a < b, 1.0, 0.0) for a in rank] for b in rank]
    rows, strip = out.shape[1:]
    for b in range(strip // LANES):
        at = pl.ds(b * LANES, LANES)
        opacity = [
            eighth_power((part[3, :, at].astype(jnp.float32) + float(HALF)) * (1.0 / TOP))
            for part in parts
        ]
        whole = opacity[0]
        for k in range(1, n):
            whole = whole + opacity[k] * (1.0 - whole)
        picture = [None] * 3
        for k in range(n):
            share = opacity[k] * (1.0 / TOP)
            for e in range(n):
                if e != k:
                    share = share * (1.0 - before[k][e] * opacity[e])
            for c in range(3):
                term = share * (parts[k][c, :, at].astype(jnp.float32) + float(HALF))
                picture[c] = term if k == 0 else picture[c] + term
        for c in range(3):
            out[c, :, at] = picture[c]
        out[3, :, at] = whole


def composite(order, parts, ks):
    n = len(parts)
    rows, strip = parts[0].shape[1:]
    return pl.pallas_call(
        functools.partial(composite_kernel, ks),
        in_specs=[SMEM] + [VMEM] * n,
        out_specs=VMEM,
        out_shape=jax.ShapeDtypeStruct((4, rows, strip), jnp.float32),
        scratch_shapes=[pltpu.SMEM((n,), jnp.int32)],
        compiler_params=pltpu.CompilerParams(vmem_limit_bytes=16 * 1024 * 1024),
        name="composite",
    )(order, *parts)


def on_device(volume, brick_mask, brick_order):
    channels, depth, rows, cols = volume.shape
    n = lax.axis_size("depth")
    assert lax.axis_size("tile") == 2
    step_size = 3.0 / (depth * n)
    mask = jnp.repeat(brick_mask, cols // brick_mask.shape[1] // LANES, axis=1)

    density, near, far, edge, mask = edges(volume, mask)
    border = lax.ppermute(edge, "tile", [(0, 1), (1, 0)])
    pairs = [(i, i ^ 1) for i in range(n) if i ^ 1 < n]
    near = lax.ppermute(near, "depth", pairs)
    pairs = [(i, i + 1) for i in range(1, n - 1, 2)]
    far = lax.ppermute(far, "depth", pairs + [(b, a) for a, b in pairs])

    first, second = rounds(n)[: n // 2] + [0], rounds(n)[n // 2 : -1]
    sums, ends = march_far(volume, density, border, mask, step_size, n, first)
    strips = finish(sums, ends, near, far, n, first)
    strips, mask = lax.optimization_barrier((strips, mask))
    strips = list(strips) + list(
        march_near(volume, density, border, near, far, mask, step_size, n, second)
    )
    parts = [
        lax.ppermute(strip, "depth", partners(n, k)) if k else strip
        for strip, k in zip(strips, first + second)
    ]
    picture = composite(brick_order, parts, first + second)
    return lax.all_gather(picture, "tile", axis=1, tiled=True)


def solution(mesh):
    return jax.shard_map(
        on_device,
        mesh=mesh,
        in_specs=(
            P(None, ("parts", "depth"), "tile", None),
            P(("parts", "depth"), None),
            P("parts"),
        ),
        out_specs=P(None, "parts", "depth"),
        check_vma=False,
    )
```

```python
import functools
import math

import jax
import jax.numpy as jnp
from jax import lax
from jax.experimental import pallas as pl
from jax.experimental.pallas import tpu as pltpu
from jax.sharding import PartitionSpec as P

LANES = 128
TOP = 65535.0
HALF = 32768
CHUNKS = 4

VMEM = pl.BlockSpec(memory_space=pltpu.VMEM)
SMEM = pl.BlockSpec(memory_space=pltpu.SMEM)
HBM = pl.BlockSpec(memory_space=pltpu.HBM)


def rounds(n):
    return list(range(n - 1, -1, -1))


def partners(n, k):
    if n & (n - 1) == 0:
        return [(i, i ^ k) for i in range(n)]
    return [(i, (i + k) % n) for i in range(n)]


def target(n, me, k):
    if n & (n - 1) == 0:
        return lax.bitwise_xor(me, k)
    return lax.rem(me + k, n)


def source(n, me, k):
    if n & (n - 1) == 0:
        return lax.bitwise_xor(me, k)
    return lax.rem(me + n - k, n)


def mask_at(mask, place, blocks):
    inside = jnp.logical_and(place >= 0, place < blocks)
    kept = mask[0, jnp.clip(place, 0, blocks - 1)]
    return jnp.where(inside, kept, 0)


def columns(place):
    return pl.ds(pl.multiple_of(place * LANES, LANES), LANES)


def edges_kernel(mask_hbm, vol, density, near, far, edge, mask, sems, mask_sem):
    depth, rows, cols = density.shape
    chunk = cols // CHUNKS
    copies = []
    for c in range(CHUNKS):
        where = pl.ds(c * chunk, chunk)
        copies.append(
            pltpu.make_async_copy(vol.at[0, :, :, where], density.at[:, :, where], sems.at[c])
        )
        copies[-1].start()
    mask_copy = pltpu.make_async_copy(mask_hbm, mask, mask_sem)
    mask_copy.start()
    row = jnp.where(lax.axis_index("tile") == 0, rows - 1, 0)
    even = lax.rem(lax.axis_index("depth"), 2) == 0
    at = lax.broadcasted_iota(jnp.int32, (depth, depth * rows), 1)
    cell = lax.broadcasted_iota(jnp.int32, (depth, depth * rows), 0)
    pick = (at == cell * rows + row).astype(jnp.bfloat16)
    mask_copy.wait()
    for b in range(cols // LANES):
        if b % (chunk // LANES) == 0:
            copies[b // (chunk // LANES)].wait()
        keep = mask[0, b].astype(jnp.float32)
        here = pl.ds(b * LANES, LANES)
        planes = density[:, :, here].reshape(depth * rows, LANES)
        border = jnp.dot(pick, planes, preferred_element_type=jnp.float32)
        edge[:, here] = (border * keep).astype(jnp.bfloat16)
        first = density[0, :, here].astype(jnp.float32) * keep
        last = density[depth - 1, :, here].astype(jnp.float32) * keep
        near[:, here] = jnp.where(even, last, first).astype(jnp.bfloat16)
        far[:, here] = jnp.where(even, first, last).astype(jnp.bfloat16)


def edges(volume, mask):
    channels, depth, rows, cols = volume.shape
    plane = jax.ShapeDtypeStruct((rows, cols), jnp.bfloat16)
    return pl.pallas_call(
        edges_kernel,
        in_specs=[HBM, HBM],
        out_specs=[VMEM] * 4 + [SMEM],
        out_shape=[
            jax.ShapeDtypeStruct((depth, rows, cols), jnp.bfloat16),
            plane,
            plane,
            jax.ShapeDtypeStruct((depth, cols), jnp.bfloat16),
            jax.ShapeDtypeStruct(mask.shape, jnp.int32),
        ],
        scratch_shapes=[pltpu.SemaphoreType.DMA((CHUNKS,)), pltpu.SemaphoreType.DMA],
        compiler_params=pltpu.CompilerParams(vmem_limit_bytes=48 * 1024 * 1024),
        cost_estimate=pl.CostEstimate(
            flops=1000000, bytes_accessed=2 * depth * rows * cols, transcendentals=0
        ),
        name="edges",
    )(mask, volume)


def shade(g_depth, flat, slope):
    return 0.3 + jnp.abs(0.28 * g_depth + slope) * lax.rsqrt(1.0 + 0.25 * (g_depth * g_depth + flat))


def halves(even, near, far, where):
    near = near[:, where].astype(jnp.float32)
    far = far[:, where].astype(jnp.float32)
    return jnp.where(even, far, near), jnp.where(even, near, far)


def march_brick(step_size, vol, density, border, mask, place, planes, put_end, put):
    depth, rows, cols = density.shape
    blocks = cols // LANES
    lane = lax.broadcasted_iota(jnp.int32, (rows, LANES), 1)
    row = lax.broadcasted_iota(jnp.int32, (rows, LANES), 0)
    first_row, last_row = row == 0, row == rows - 1
    first_lane, last_lane = lane == 0, lane == LANES - 1
    right_half = lane >= LANES // 2
    rate = -step_size * math.log2(math.e)
    to_top = lax.axis_index("tile").astype(jnp.float32)
    here_at = columns(place)
    left_at = columns(jnp.maximum(place - 1, 0))
    right_at = columns(jnp.minimum(place + 1, blocks - 1))
    keep_left = mask_at(mask, place - 1, blocks).astype(jnp.float32)
    keep_right = mask_at(mask, place + 1, blocks).astype(jnp.float32)
    keep_side = jnp.where(right_half, keep_left, keep_right)
    halo = border[:, here_at].astype(jnp.float32)
    top, bottom = halo * to_top, halo * (1.0 - to_top)
    zeros = jnp.zeros((rows, LANES), jnp.float32)
    total, clear, plain = zeros, jnp.ones((rows, LANES), jnp.float32), zeros
    sums = [zeros for _ in range(3)]
    before = planes[0] if planes else None
    here = density[0, :, here_at].astype(jnp.float32)
    for d in range(depth):
        if d + 1 < depth:
            after = density[d + 1, :, here_at].astype(jnp.float32)
        else:
            after = planes[1] if planes else None
        left = density[d, :, left_at].astype(jnp.float32)
        right = density[d, :, right_at].astype(jnp.float32)
        side = jnp.where(right_half, left, right) * keep_side
        less = pltpu.roll(jnp.where(last_lane, side, here), 1, 1)
        more = pltpu.roll(jnp.where(first_lane, side, here), LANES - 1, 1)
        up = jnp.where(first_row, top[d : d + 1], pltpu.roll(here, 1, 0))
        down = jnp.where(last_row, bottom[d : d + 1], pltpu.roll(here, rows - 1, 0))
        g_rows, g_cols = down - up, more - less
        flat = g_rows * g_rows + g_cols * g_cols
        slope = 0.126 * g_rows + 0.168 * g_cols
        total = total + here * here
        left_over = jnp.exp2(total * rate)
        weight = clear - left_over
        clear = left_over
        glow = [jnp.tanh(0.5 * vol[1 + k, d, :, here_at].astype(jnp.float32)) for k in range(3)]
        if before is None or after is None:
            inner = after if before is None else before
            half = 0.5 * weight
            put_end(0 if d == 0 else 1, [inner, flat, slope] + [half + half * g for g in glow])
        else:
            weight = weight * shade(after - before, flat, slope)
            plain = plain + weight
            for k in range(3):
                sums[k] = sums[k] + weight * glow[k]
        before, here = here, after
    put([0.5 * (plain + sums[k]) for k in range(3)], clear)


def encode(out, there, colours, clear):
    root = jnp.sqrt(jnp.sqrt(jnp.sqrt(1.0 - clear)))
    level = (root * TOP + 0.5).astype(jnp.int32)
    out[3, :, there] = (level - HALF).astype(jnp.int16)
    gain = TOP / jnp.maximum(eighth_power(level.astype(jnp.float32) * (1.0 / TOP)), 1e-30)
    for k in range(3):
        level = jnp.minimum(colours[k] * gain + 0.5, TOP)
        out[k, :, there] = (level.astype(jnp.int32) - HALF).astype(jnp.int16)


def eighth_power(root):
    square = root * root
    square = square * square
    return square * square


def far_kernel(step_size, n, ks, mask, vol, density, border, sums_out, ends):
    depth, rows, cols = density.shape
    bricks = cols // LANES // n
    me = lax.axis_index("depth")

    def step(i, carry):
        place = target(n, me, lax.select(i // bricks < n // 2, n - 1 - i // bricks, 0)) * bricks + i % bricks
        here = columns(i)

        def put_end(end, values):
            for v, value in enumerate(values):
                ends[end, v, :, here] = value

        def put(colours, clear):
            for v, value in enumerate(colours + [clear]):
                sums_out[v, :, here] = value

        keep = mask[0, place] != 0

        @pl.when(keep)
        def _():
            march_brick(
                step_size, vol, density, border, mask, place, None, put_end, put
            )

        @pl.when(jnp.logical_not(keep))
        def _():
            empty = jnp.zeros((rows, LANES), jnp.float32)
            put([empty] * 3, empty + 1.0)
            put_end(0, [empty] * 6)
            put_end(1, [empty] * 6)

        return carry

    lax.fori_loop(0, len(ks) * bricks, step, 0)


def costs(cells):
    return pl.CostEstimate(flops=40 * cells, bytes_accessed=8 * cells, transcendentals=5 * cells)


def march_far(volume, density, border, mask, step_size, n, ks):
    channels, depth, rows, cols = volume.shape
    width = cols // n * len(ks)
    return pl.pallas_call(
        functools.partial(far_kernel, step_size, n, ks),
        in_specs=[SMEM, VMEM, VMEM, VMEM],
        out_specs=[VMEM] * 2,
        out_shape=[
            jax.ShapeDtypeStruct((4, rows, width), jnp.float32),
            jax.ShapeDtypeStruct((2, 6, rows, width), jnp.float32),
        ],
        cost_estimate=costs(depth * rows * width),
        compiler_params=pltpu.CompilerParams(vmem_limit_bytes=20 * 1024 * 1024),
        name="march_far",
    )(mask, volume, density, border)


def finish_kernel(n, ks, sums, ends, near, far, *outs):
    rows, cols = near.shape
    strip = cols // n
    width = math.gcd(strip, 2 * LANES)
    me = lax.axis_index("depth")
    even = lax.rem(me, 2) == 0
    for j, k in enumerate(ks):
        at = target(n, me, k) * strip
        for c in range(strip // width):
            here = pl.ds(j * strip + c * width, width)
            planes = halves(
                even, near, far, pl.ds(pl.multiple_of(at + c * width, LANES), width)
            )
            colours = [sums[v, :, here] for v in range(3)]
            for end in range(2):
                g_depth = ends[end, 0, :, here] - planes[end]
                if end == 1:
                    g_depth = -g_depth
                shading = shade(g_depth, ends[end, 1, :, here], ends[end, 2, :, here])
                for v in range(3):
                    colours[v] = colours[v] + shading * ends[end, 3 + v, :, here]
            encode(outs[j], pl.ds(c * width, width), colours, sums[3, :, here])


def finish(sums, ends, near, far, n, ks):
    rows, cols = near.shape
    cells = rows * cols // n * len(ks)
    return pl.pallas_call(
        functools.partial(finish_kernel, n, ks),
        in_specs=[VMEM] * 4,
        out_specs=[VMEM] * len(ks),
        out_shape=[jax.ShapeDtypeStruct((4, rows, cols // n), jnp.int16)] * len(ks),
        cost_estimate=pl.CostEstimate(
            flops=60 * cells, bytes_accessed=64 * cells, transcendentals=4 * cells
        ),
        compiler_params=pltpu.CompilerParams(vmem_limit_bytes=16 * 1024 * 1024),
        name="finish",
    )(sums, ends, near, far)


def near_kernel(step_size, n, ks, mask, vol, density, border, near, far, *outs):
    depth, rows, cols = density.shape
    bricks = cols // LANES // n
    me = lax.axis_index("depth")
    even = lax.rem(me, 2) == 0
    for k, out in zip(ks, outs):
        at = target(n, me, k)

        def step(b, carry, at=at, out=out):
            place = at * bricks + b
            there = columns(b)
            keep = mask[0, place] != 0

            @pl.when(keep)
            def _():
                planes = halves(even, near, far, columns(place))

                def put(colours, clear):
                    encode(out, there, colours, clear)

                march_brick(
                    step_size, vol, density, border, mask, place, planes, None, put
                )

            @pl.when(jnp.logical_not(keep))
            def _():
                low = jnp.full((rows, LANES), -HALF, jnp.int32).astype(jnp.int16)
                for c in range(4):
                    out[c, :, there] = low

            return carry

        lax.fori_loop(0, bricks, step, 0)


def march_near(volume, density, border, near, far, mask, step_size, n, ks):
    channels, depth, rows, cols = volume.shape
    width = cols // n * len(ks)
    return pl.pallas_call(
        functools.partial(near_kernel, step_size, n, ks),
        in_specs=[SMEM] + [VMEM] * 5,
        out_specs=[VMEM] * len(ks),
        out_shape=[jax.ShapeDtypeStruct((4, rows, cols // n), jnp.int16)] * len(ks),
        cost_estimate=costs(depth * rows * width),
        compiler_params=pltpu.CompilerParams(vmem_limit_bytes=20 * 1024 * 1024),
        name="march_near",
    )(mask, volume, density, border, near, far)


def composite_kernel(ks, order, *refs):
    n = len(ks)
    parts, out = refs[:n], refs[n]
    me = lax.axis_index("depth")
    place = lax.broadcasted_iota(jnp.int32, order.shape, 1).astype(jnp.float32)
    slabs = order[...]
    rank = [
        jnp.sum(jnp.where(slabs == source(n, me, k), place, 0.0), axis=1, keepdims=True)
        for k in ks
    ]
    before = [[jnp.where(a < b, 1.0, 0.0) for a in rank] for b in rank]
    rows, strip = out.shape[1:]
    for b in range(strip // LANES):
        at = pl.ds(b * LANES, LANES)
        opacity = [
            eighth_power((part[3, :, at].astype(jnp.float32) + float(HALF)) * (1.0 / TOP))
            for part in parts
        ]
        whole = opacity[0]
        for k in range(1, n):
            whole = whole + opacity[k] * (1.0 - whole)
        picture = [None] * 3
        for k in range(n):
            share = opacity[k] * (1.0 / TOP)
            for e in range(n):
                if e != k:
                    share = share * (1.0 - before[k][e] * opacity[e])
            for c in range(3):
                term = share * (parts[k][c, :, at].astype(jnp.float32) + float(HALF))
                picture[c] = term if k == 0 else picture[c] + term
        for c in range(3):
            out[c, :, at] = picture[c]
        out[3, :, at] = whole


def composite(order, parts, ks):
    n = len(parts)
    rows, strip = parts[0].shape[1:]
    return pl.pallas_call(
        functools.partial(composite_kernel, ks),
        in_specs=[VMEM] * (n + 1),
        out_specs=VMEM,
        out_shape=jax.ShapeDtypeStruct((4, rows, strip), jnp.float32),
        compiler_params=pltpu.CompilerParams(vmem_limit_bytes=16 * 1024 * 1024),
        name="composite",
    )(order.reshape(1, n), *parts)


def on_device(volume, brick_mask, brick_order):
    channels, depth, rows, cols = volume.shape
    n = lax.axis_size("depth")
    assert lax.axis_size("tile") == 2
    step_size = 3.0 / (depth * n)
    mask = jnp.repeat(brick_mask, cols // brick_mask.shape[1] // LANES, axis=1)

    density, near, far, edge, mask = edges(volume, mask)
    border = lax.ppermute(edge, "tile", [(0, 1), (1, 0)])
    pairs = [(i, i ^ 1) for i in range(n) if i ^ 1 < n]
    near = lax.ppermute(near, "depth", pairs)
    pairs = [(i, i + 1) for i in range(1, n - 1, 2)]
    far = lax.ppermute(far, "depth", pairs + [(b, a) for a, b in pairs])

    first, second = rounds(n)[: n // 2] + [0], rounds(n)[n // 2 : -1]
    sums, ends = march_far(volume, density, border, mask, step_size, n, first)
    strips = finish(sums, ends, near, far, n, first)
    strips, mask = lax.optimization_barrier((strips, mask))
    strips = list(strips) + list(
        march_near(volume, density, border, near, far, mask, step_size, n, second)
    )
    parts = [
        lax.ppermute(strip, "depth", partners(n, k)) if k else strip
        for strip, k in zip(strips, first + second)
    ]
    picture = composite(brick_order, parts, first + second)
    return lax.all_gather(picture, "tile", axis=1, tiled=True)


def solution(mesh):
    return jax.shard_map(
        on_device,
        mesh=mesh,
        in_specs=(
            P(None, ("parts", "depth"), "tile", None),
            P(("parts", "depth"), None),
            P("parts"),
        ),
        out_specs=P(None, "parts", "depth"),
        check_vma=False,
    )
```

```python
import functools
import math

import jax
import jax.numpy as jnp
from jax import lax
from jax.experimental import pallas as pl
from jax.experimental.pallas import tpu as pltpu
from jax.sharding import PartitionSpec as P

LANES = 128
TOP = 65535.0
HALF = 32768
CHUNKS = 4

VMEM = pl.BlockSpec(memory_space=pltpu.VMEM)
SMEM = pl.BlockSpec(memory_space=pltpu.SMEM)
HBM = pl.BlockSpec(memory_space=pltpu.HBM)


def rounds(n):
    return list(range(n - 1, -1, -1))


def partners(n, k):
    if n & (n - 1) == 0:
        return [(i, i ^ k) for i in range(n)]
    return [(i, (i + k) % n) for i in range(n)]


def target(n, me, k):
    if n & (n - 1) == 0:
        return lax.bitwise_xor(me, k)
    return lax.rem(me + k, n)


def source(n, me, k):
    if n & (n - 1) == 0:
        return lax.bitwise_xor(me, k)
    return lax.rem(me + n - k, n)


def mask_at(mask, place, blocks):
    inside = jnp.logical_and(place >= 0, place < blocks)
    kept = mask[0, jnp.clip(place, 0, blocks - 1)]
    return jnp.where(inside, kept, 0)


def columns(place):
    return pl.ds(pl.multiple_of(place * LANES, LANES), LANES)


def edges_kernel(mask_hbm, vol, density, near, far, edge, mask, sems, mask_sem):
    depth, rows, cols = density.shape
    chunk = cols // CHUNKS
    copies = []
    for c in range(CHUNKS):
        where = pl.ds(c * chunk, chunk)
        copies.append(
            pltpu.make_async_copy(vol.at[0, :, :, where], density.at[:, :, where], sems.at[c])
        )
        copies[-1].start()
    mask_copy = pltpu.make_async_copy(mask_hbm, mask, mask_sem)
    mask_copy.start()
    row = jnp.where(lax.axis_index("tile") == 0, rows - 1, 0)
    even = lax.rem(lax.axis_index("depth"), 2) == 0
    at = lax.broadcasted_iota(jnp.int32, (depth, depth * rows), 1)
    cell = lax.broadcasted_iota(jnp.int32, (depth, depth * rows), 0)
    pick = (at == cell * rows + row).astype(jnp.bfloat16)
    mask_copy.wait()
    for b in range(cols // LANES):
        if b % (chunk // LANES) == 0:
            copies[b // (chunk // LANES)].wait()
        keep = mask[0, b].astype(jnp.float32)
        here = pl.ds(b * LANES, LANES)
        planes = density[:, :, here].reshape(depth * rows, LANES)
        border = jnp.dot(pick, planes, preferred_element_type=jnp.float32)
        edge[:, here] = (border * keep).astype(jnp.bfloat16)
        first = density[0, :, here].astype(jnp.float32) * keep
        last = density[depth - 1, :, here].astype(jnp.float32) * keep
        near[:, here] = jnp.where(even, last, first).astype(jnp.bfloat16)
        far[:, here] = jnp.where(even, first, last).astype(jnp.bfloat16)


def edges(volume, mask):
    channels, depth, rows, cols = volume.shape
    plane = jax.ShapeDtypeStruct((rows, cols), jnp.bfloat16)
    return pl.pallas_call(
        edges_kernel,
        in_specs=[HBM, HBM],
        out_specs=[VMEM] * 4 + [SMEM],
        out_shape=[
            jax.ShapeDtypeStruct((depth, rows, cols), jnp.bfloat16),
            plane,
            plane,
            jax.ShapeDtypeStruct((depth, cols), jnp.bfloat16),
            jax.ShapeDtypeStruct(mask.shape, jnp.int32),
        ],
        scratch_shapes=[pltpu.SemaphoreType.DMA((CHUNKS,)), pltpu.SemaphoreType.DMA],
        compiler_params=pltpu.CompilerParams(vmem_limit_bytes=48 * 1024 * 1024),
        cost_estimate=pl.CostEstimate(
            flops=1000000, bytes_accessed=2 * depth * rows * cols, transcendentals=0
        ),
        name="edges",
    )(mask, volume)


def shade(g_depth, flat, slope):
    return 0.3 + jnp.abs(0.28 * g_depth + slope) * lax.rsqrt(1.0 + 0.25 * (g_depth * g_depth + flat))


def halves(even, near, far, where):
    near = near[:, where].astype(jnp.float32)
    far = far[:, where].astype(jnp.float32)
    return jnp.where(even, far, near), jnp.where(even, near, far)


def march_brick(step_size, vol, density, border, mask, place, planes, put_end, put):
    depth, rows, cols = density.shape
    blocks = cols // LANES
    lane = lax.broadcasted_iota(jnp.int32, (rows, LANES), 1)
    row = lax.broadcasted_iota(jnp.int32, (rows, LANES), 0)
    first_row, last_row = row == 0, row == rows - 1
    first_lane, last_lane = lane == 0, lane == LANES - 1
    right_half = lane >= LANES // 2
    rate = -step_size * math.log2(math.e)
    to_top = lax.axis_index("tile").astype(jnp.float32)
    here_at = columns(place)
    left_at = columns(jnp.maximum(place - 1, 0))
    right_at = columns(jnp.minimum(place + 1, blocks - 1))
    keep_left = mask_at(mask, place - 1, blocks).astype(jnp.float32)
    keep_right = mask_at(mask, place + 1, blocks).astype(jnp.float32)
    keep_side = jnp.where(right_half, keep_left, keep_right)
    halo = border[:, here_at].astype(jnp.float32)
    top, bottom = halo * to_top, halo * (1.0 - to_top)
    zeros = jnp.zeros((rows, LANES), jnp.float32)
    total, clear, plain = zeros, jnp.ones((rows, LANES), jnp.float32), zeros
    sums = [zeros for _ in range(3)]
    before = planes[0] if planes else None
    here = density[0, :, here_at].astype(jnp.float32)
    for d in range(depth):
        if d + 1 < depth:
            after = density[d + 1, :, here_at].astype(jnp.float32)
        else:
            after = planes[1] if planes else None
        left = density[d, :, left_at].astype(jnp.float32)
        right = density[d, :, right_at].astype(jnp.float32)
        side = jnp.where(right_half, left, right) * keep_side
        less = pltpu.roll(jnp.where(last_lane, side, here), 1, 1)
        more = pltpu.roll(jnp.where(first_lane, side, here), LANES - 1, 1)
        up = jnp.where(first_row, top[d : d + 1], pltpu.roll(here, 1, 0))
        down = jnp.where(last_row, bottom[d : d + 1], pltpu.roll(here, rows - 1, 0))
        g_rows, g_cols = down - up, more - less
        flat = g_rows * g_rows + g_cols * g_cols
        slope = 0.126 * g_rows + 0.168 * g_cols
        total = total + here * here
        left_over = jnp.exp2(total * rate)
        weight = clear - left_over
        clear = left_over
        glow = [jnp.tanh(0.5 * vol[1 + k, d, :, here_at].astype(jnp.float32)) for k in range(3)]
        if before is None or after is None:
            inner = after if before is None else before
            half = 0.5 * weight
            put_end(0 if d == 0 else 1, [inner, flat, slope] + [half + half * g for g in glow])
        else:
            weight = weight * shade(after - before, flat, slope)
            plain = plain + weight
            for k in range(3):
                sums[k] = sums[k] + weight * glow[k]
        before, here = here, after
    put([0.5 * (plain + sums[k]) for k in range(3)], total * step_size)


def encode(out, there, colours, optical):
    thin = optical * (1.0 - optical * (0.5 - optical * (1.0 / 6.0 - optical * (1.0 / 24.0))))
    opacity = jnp.where(optical < 0.03, thin, 1.0 - jnp.exp(-optical))
    root = jnp.sqrt(jnp.sqrt(jnp.sqrt(opacity)))
    level = (root * TOP + 0.5).astype(jnp.int32)
    out[3, :, there] = (level - HALF).astype(jnp.int16)
    gain = TOP / jnp.maximum(eighth_power(level.astype(jnp.float32) * (1.0 / TOP)), 1e-30)
    for k in range(3):
        level = jnp.minimum(colours[k] * gain + 0.5, TOP)
        out[k, :, there] = (level.astype(jnp.int32) - HALF).astype(jnp.int16)


def eighth_power(root):
    square = root * root
    square = square * square
    return square * square


def far_kernel(step_size, n, ks, mask, vol, density, border, sums_out, ends):
    depth, rows, cols = density.shape
    bricks = cols // LANES // n
    me = lax.axis_index("depth")

    def step(i, carry):
        place = target(n, me, lax.select(i // bricks < n // 2, n - 1 - i // bricks, 0)) * bricks + i % bricks
        here = columns(i)

        def put_end(end, values):
            for v, value in enumerate(values):
                ends[end, v, :, here] = value

        def put(colours, optical):
            for v, value in enumerate(colours + [optical]):
                sums_out[v, :, here] = value

        keep = mask[0, place] != 0

        @pl.when(keep)
        def _():
            march_brick(
                step_size, vol, density, border, mask, place, None, put_end, put
            )

        @pl.when(jnp.logical_not(keep))
        def _():
            empty = jnp.zeros((rows, LANES), jnp.float32)
            put([empty] * 3, empty)
            put_end(0, [empty] * 6)
            put_end(1, [empty] * 6)

        return carry

    lax.fori_loop(0, len(ks) * bricks, step, 0)


def costs(cells):
    return pl.CostEstimate(flops=40 * cells, bytes_accessed=8 * cells, transcendentals=5 * cells)


def march_far(volume, density, border, mask, step_size, n, ks):
    channels, depth, rows, cols = volume.shape
    width = cols // n * len(ks)
    return pl.pallas_call(
        functools.partial(far_kernel, step_size, n, ks),
        in_specs=[SMEM, VMEM, VMEM, VMEM],
        out_specs=[VMEM] * 2,
        out_shape=[
            jax.ShapeDtypeStruct((4, rows, width), jnp.float32),
            jax.ShapeDtypeStruct((2, 6, rows, width), jnp.float32),
        ],
        cost_estimate=costs(depth * rows * width),
        compiler_params=pltpu.CompilerParams(vmem_limit_bytes=20 * 1024 * 1024),
        name="march_far",
    )(mask, volume, density, border)


def finish_kernel(n, ks, sums, ends, near, far, *outs):
    rows, cols = near.shape
    strip = cols // n
    width = math.gcd(strip, 2 * LANES)
    me = lax.axis_index("depth")
    even = lax.rem(me, 2) == 0
    for j, k in enumerate(ks):
        at = target(n, me, k) * strip
        for c in range(strip // width):
            here = pl.ds(j * strip + c * width, width)
            planes = halves(
                even, near, far, pl.ds(pl.multiple_of(at + c * width, LANES), width)
            )
            colours = [sums[v, :, here] for v in range(3)]
            for end in range(2):
                g_depth = ends[end, 0, :, here] - planes[end]
                if end == 1:
                    g_depth = -g_depth
                shading = shade(g_depth, ends[end, 1, :, here], ends[end, 2, :, here])
                for v in range(3):
                    colours[v] = colours[v] + shading * ends[end, 3 + v, :, here]
            encode(outs[j], pl.ds(c * width, width), colours, sums[3, :, here])


def finish(sums, ends, near, far, n, ks):
    rows, cols = near.shape
    cells = rows * cols // n * len(ks)
    return pl.pallas_call(
        functools.partial(finish_kernel, n, ks),
        in_specs=[VMEM] * 4,
        out_specs=[VMEM] * len(ks),
        out_shape=[jax.ShapeDtypeStruct((4, rows, cols // n), jnp.int16)] * len(ks),
        cost_estimate=pl.CostEstimate(
            flops=60 * cells, bytes_accessed=64 * cells, transcendentals=4 * cells
        ),
        compiler_params=pltpu.CompilerParams(vmem_limit_bytes=16 * 1024 * 1024),
        name="finish",
    )(sums, ends, near, far)


def near_kernel(step_size, n, ks, mask, vol, density, border, near, far, *outs):
    depth, rows, cols = density.shape
    bricks = cols // LANES // n
    me = lax.axis_index("depth")
    even = lax.rem(me, 2) == 0
    for k, out in zip(ks, outs):
        at = target(n, me, k)

        def step(b, carry, at=at, out=out):
            place = at * bricks + b
            there = columns(b)
            keep = mask[0, place] != 0

            @pl.when(keep)
            def _():
                planes = halves(even, near, far, columns(place))

                def put(colours, optical):
                    encode(out, there, colours, optical)

                march_brick(
                    step_size, vol, density, border, mask, place, planes, None, put
                )

            @pl.when(jnp.logical_not(keep))
            def _():
                low = jnp.full((rows, LANES), -HALF, jnp.int32).astype(jnp.int16)
                for c in range(4):
                    out[c, :, there] = low

            return carry

        lax.fori_loop(0, bricks, step, 0)


def march_near(volume, density, border, near, far, mask, step_size, n, ks):
    channels, depth, rows, cols = volume.shape
    width = cols // n * len(ks)
    return pl.pallas_call(
        functools.partial(near_kernel, step_size, n, ks),
        in_specs=[SMEM] + [VMEM] * 5,
        out_specs=[VMEM] * len(ks),
        out_shape=[jax.ShapeDtypeStruct((4, rows, cols // n), jnp.int16)] * len(ks),
        cost_estimate=costs(depth * rows * width),
        compiler_params=pltpu.CompilerParams(vmem_limit_bytes=20 * 1024 * 1024),
        name="march_near",
    )(mask, volume, density, border, near, far)


def composite_kernel(ks, order, *refs):
    n = len(ks)
    parts, out = refs[:n], refs[n]
    me = lax.axis_index("depth")
    place = lax.broadcasted_iota(jnp.int32, order.shape, 1).astype(jnp.float32)
    slabs = order[...]
    rank = [
        jnp.sum(jnp.where(slabs == source(n, me, k), place, 0.0), axis=1, keepdims=True)
        for k in ks
    ]
    before = [[jnp.where(a < b, 1.0, 0.0) for a in rank] for b in rank]
    rows, strip = out.shape[1:]
    for b in range(strip // LANES):
        at = pl.ds(b * LANES, LANES)
        opacity = [
            eighth_power((part[3, :, at].astype(jnp.float32) + float(HALF)) * (1.0 / TOP))
            for part in parts
        ]
        whole = opacity[0]
        for k in range(1, n):
            whole = whole + opacity[k] * (1.0 - whole)
        picture = [None] * 3
        for k in range(n):
            share = opacity[k] * (1.0 / TOP)
            for e in range(n):
                if e != k:
                    share = share * (1.0 - before[k][e] * opacity[e])
            for c in range(3):
                term = share * (parts[k][c, :, at].astype(jnp.float32) + float(HALF))
                picture[c] = term if k == 0 else picture[c] + term
        for c in range(3):
            out[c, :, at] = picture[c]
        out[3, :, at] = whole


def composite(order, parts, ks):
    n = len(parts)
    rows, strip = parts[0].shape[1:]
    return pl.pallas_call(
        functools.partial(composite_kernel, ks),
        in_specs=[VMEM] * (n + 1),
        out_specs=VMEM,
        out_shape=jax.ShapeDtypeStruct((4, rows, strip), jnp.float32),
        compiler_params=pltpu.CompilerParams(vmem_limit_bytes=16 * 1024 * 1024),
        name="composite",
    )(order.reshape(1, n), *parts)


def on_device(volume, brick_mask, brick_order):
    channels, depth, rows, cols = volume.shape
    n = lax.axis_size("depth")
    assert lax.axis_size("tile") == 2
    step_size = 3.0 / (depth * n)
    mask = jnp.repeat(brick_mask, cols // brick_mask.shape[1] // LANES, axis=1)

    density, near, far, edge, mask = edges(volume, mask)
    border = lax.ppermute(edge, "tile", [(0, 1), (1, 0)])
    pairs = [(i, i ^ 1) for i in range(n) if i ^ 1 < n]
    near = lax.ppermute(near, "depth", pairs)
    pairs = [(i, i + 1) for i in range(1, n - 1, 2)]
    far = lax.ppermute(far, "depth", pairs + [(b, a) for a, b in pairs])

    first, second = rounds(n)[: n // 2] + [0], rounds(n)[n // 2 : -1]
    sums, ends = march_far(volume, density, border, mask, step_size, n, first)
    strips = finish(sums, ends, near, far, n, first)
    strips, mask = lax.optimization_barrier((strips, mask))
    strips = list(strips) + list(
        march_near(volume, density, border, near, far, mask, step_size, n, second)
    )
    parts = [
        lax.ppermute(strip, "depth", partners(n, k)) if k else strip
        for strip, k in zip(strips, first + second)
    ]
    picture = composite(brick_order, parts, first + second)
    return lax.all_gather(picture, "tile", axis=1, tiled=True)


def solution(mesh):
    return jax.shard_map(
        on_device,
        mesh=mesh,
        in_specs=(
            P(None, ("parts", "depth"), "tile", None),
            P(("parts", "depth"), None),
            P("parts"),
        ),
        out_specs=P(None, "parts", "depth"),
        check_vma=False,
    )
```

```python
import functools
import math

import jax
import jax.numpy as jnp
from jax import lax
from jax.experimental import pallas as pl
from jax.experimental.pallas import tpu as pltpu
from jax.sharding import PartitionSpec as P

LANES = 128
TOP = 65535.0
HALF = 32768
CHUNKS = 4

VMEM = pl.BlockSpec(memory_space=pltpu.VMEM)
SMEM = pl.BlockSpec(memory_space=pltpu.SMEM)
HBM = pl.BlockSpec(memory_space=pltpu.HBM)


def rounds(n):
    return list(range(n - 1, -1, -1))


def partners(n, k):
    if n & (n - 1) == 0:
        return [(i, i ^ k) for i in range(n)]
    return [(i, (i + k) % n) for i in range(n)]


def target(n, me, k):
    if n & (n - 1) == 0:
        return lax.bitwise_xor(me, k)
    return lax.rem(me + k, n)


def source(n, me, k):
    if n & (n - 1) == 0:
        return lax.bitwise_xor(me, k)
    return lax.rem(me + n - k, n)


def mask_at(mask, place, blocks):
    inside = jnp.logical_and(place >= 0, place < blocks)
    kept = mask[0, jnp.clip(place, 0, blocks - 1)]
    return jnp.where(inside, kept, 0)


def columns(place):
    return pl.ds(pl.multiple_of(place * LANES, LANES), LANES)


def edges_kernel(mask_hbm, vol, density, near, far, edge, mask, sems, mask_sem):
    depth, rows, cols = density.shape
    chunk = cols // CHUNKS
    copies = []
    for c in range(CHUNKS):
        where = pl.ds(c * chunk, chunk)
        copies.append(
            pltpu.make_async_copy(vol.at[0, :, :, where], density.at[:, :, where], sems.at[c])
        )
        copies[-1].start()
    mask_copy = pltpu.make_async_copy(mask_hbm, mask, mask_sem)
    mask_copy.start()
    row = jnp.where(lax.axis_index("tile") == 0, rows - 1, 0)
    even = lax.rem(lax.axis_index("depth"), 2) == 0
    at = lax.broadcasted_iota(jnp.int32, (depth, depth * rows), 1)
    cell = lax.broadcasted_iota(jnp.int32, (depth, depth * rows), 0)
    pick = (at == cell * rows + row).astype(jnp.bfloat16)
    mask_copy.wait()
    for b in range(cols // LANES):
        if b % (chunk // LANES) == 0:
            copies[b // (chunk // LANES)].wait()
        keep = mask[0, b].astype(jnp.float32)
        here = pl.ds(b * LANES, LANES)
        planes = density[:, :, here].reshape(depth * rows, LANES)
        border = jnp.dot(pick, planes, preferred_element_type=jnp.float32)
        edge[:, here] = (border * keep).astype(jnp.bfloat16)
        first = density[0, :, here].astype(jnp.float32) * keep
        last = density[depth - 1, :, here].astype(jnp.float32) * keep
        near[:, here] = jnp.where(even, last, first).astype(jnp.bfloat16)
        far[:, here] = jnp.where(even, first, last).astype(jnp.bfloat16)


def edges(volume, mask):
    channels, depth, rows, cols = volume.shape
    plane = jax.ShapeDtypeStruct((rows, cols), jnp.bfloat16)
    return pl.pallas_call(
        edges_kernel,
        in_specs=[HBM, HBM],
        out_specs=[VMEM] * 4 + [SMEM],
        out_shape=[
            jax.ShapeDtypeStruct((depth, rows, cols), jnp.bfloat16),
            plane,
            plane,
            jax.ShapeDtypeStruct((depth, cols), jnp.bfloat16),
            jax.ShapeDtypeStruct(mask.shape, jnp.int32),
        ],
        scratch_shapes=[pltpu.SemaphoreType.DMA((CHUNKS,)), pltpu.SemaphoreType.DMA],
        compiler_params=pltpu.CompilerParams(vmem_limit_bytes=48 * 1024 * 1024),
        cost_estimate=pl.CostEstimate(
            flops=1000000, bytes_accessed=2 * depth * rows * cols, transcendentals=0
        ),
        name="edges",
    )(mask, volume)


def shade(g_depth, flat, slope):
    return 0.3 + jnp.abs(0.28 * g_depth + slope) * lax.rsqrt(1.0 + 0.25 * (g_depth * g_depth + flat))


def halves(even, near, far, where):
    near = near[:, where].astype(jnp.float32)
    far = far[:, where].astype(jnp.float32)
    return jnp.where(even, far, near), jnp.where(even, near, far)


def march_brick(step_size, vol, density, border, mask, place, planes, put_end, put):
    depth, rows, cols = density.shape
    blocks = cols // LANES
    lane = lax.broadcasted_iota(jnp.int32, (rows, LANES), 1)
    row = lax.broadcasted_iota(jnp.int32, (rows, LANES), 0)
    first_row, last_row = row == 0, row == rows - 1
    first_lane, last_lane = lane == 0, lane == LANES - 1
    right_half = lane >= LANES // 2
    rate = -step_size * math.log2(math.e)
    to_top = lax.axis_index("tile").astype(jnp.float32)
    here_at = columns(place)
    left_at = columns(jnp.maximum(place - 1, 0))
    right_at = columns(jnp.minimum(place + 1, blocks - 1))
    keep_left = mask_at(mask, place - 1, blocks).astype(jnp.float32)
    keep_right = mask_at(mask, place + 1, blocks).astype(jnp.float32)
    keep_side = jnp.where(right_half, keep_left, keep_right)
    halo = border[:, here_at].astype(jnp.float32)
    top, bottom = halo * to_top, halo * (1.0 - to_top)
    zeros = jnp.zeros((rows, LANES), jnp.float32)
    total, clear, plain = zeros, jnp.ones((rows, LANES), jnp.float32), zeros
    sums = [zeros for _ in range(3)]
    before = planes[0] if planes else None
    here = density[0, :, here_at].astype(jnp.float32)
    for d in range(depth):
        if d + 1 < depth:
            after = density[d + 1, :, here_at].astype(jnp.float32)
        else:
            after = planes[1] if planes else None
        left = density[d, :, left_at].astype(jnp.float32)
        right = density[d, :, right_at].astype(jnp.float32)
        side = jnp.where(right_half, left, right) * keep_side
        less = pltpu.roll(jnp.where(last_lane, side, here), 1, 1)
        more = pltpu.roll(jnp.where(first_lane, side, here), LANES - 1, 1)
        up = jnp.where(first_row, top[d : d + 1], pltpu.roll(here, 1, 0))
        down = jnp.where(last_row, bottom[d : d + 1], pltpu.roll(here, rows - 1, 0))
        g_rows, g_cols = down - up, more - less
        flat = g_rows * g_rows + g_cols * g_cols
        slope = 0.126 * g_rows + 0.168 * g_cols
        total = total + here * here
        left_over = jnp.exp2(total * rate)
        weight = clear - left_over
        clear = left_over
        glow = [jnp.tanh(0.5 * vol[1 + k, d, :, here_at].astype(jnp.float32)) for k in range(3)]
        if before is None or after is None:
            inner = after if before is None else before
            half = 0.5 * weight
            put_end(0 if d == 0 else 1, [inner, flat, slope] + [half + half * g for g in glow])
        else:
            weight = weight * shade(after - before, flat, slope)
            plain = plain + weight
            for k in range(3):
                sums[k] = sums[k] + weight * glow[k]
        before, here = here, after
    put([0.5 * (plain + sums[k]) for k in range(3)], total * step_size)


def encode(out, there, colours, optical):
    thin = optical * (1.0 - optical * (0.5 - optical * (1.0 / 6.0 - optical * (1.0 / 24.0))))
    opacity = jnp.where(optical < 0.03, thin, 1.0 - jnp.exp(-optical))
    root = jnp.sqrt(jnp.sqrt(jnp.sqrt(opacity)))
    level = (root * TOP + 0.5).astype(jnp.int32)
    out[3, :, there] = (level - HALF).astype(jnp.int16)
    gain = TOP / jnp.maximum(eighth_power(level.astype(jnp.float32) * (1.0 / TOP)), 1e-30)
    for k in range(3):
        level = jnp.minimum(colours[k] * gain + 0.5, TOP)
        out[k, :, there] = (level.astype(jnp.int32) - HALF).astype(jnp.int16)


def eighth_power(root):
    square = root * root
    square = square * square
    return square * square


def far_kernel(step_size, n, ks, mask, vol, density, border, sums_out, ends):
    depth, rows, cols = density.shape
    bricks = cols // LANES // n
    me = lax.axis_index("depth")

    def step(i, carry):
        place = target(n, me, lax.select(i // bricks < n // 2, lax.bitwise_xor(n - 1 - i // bricks, n // 4), 0)) * bricks + i % bricks
        here = columns(i)

        def put_end(end, values):
            for v, value in enumerate(values):
                ends[end, v, :, here] = value

        def put(colours, optical):
            for v, value in enumerate(colours + [optical]):
                sums_out[v, :, here] = value

        keep = mask[0, place] != 0

        @pl.when(keep)
        def _():
            march_brick(
                step_size, vol, density, border, mask, place, None, put_end, put
            )

        @pl.when(jnp.logical_not(keep))
        def _():
            empty = jnp.zeros((rows, LANES), jnp.float32)
            put([empty] * 3, empty)
            put_end(0, [empty] * 6)
            put_end(1, [empty] * 6)

        return carry

    lax.fori_loop(0, len(ks) * bricks, step, 0)


def costs(cells):
    return pl.CostEstimate(flops=40 * cells, bytes_accessed=8 * cells, transcendentals=5 * cells)


def march_far(volume, density, border, mask, step_size, n, ks):
    channels, depth, rows, cols = volume.shape
    width = cols // n * len(ks)
    return pl.pallas_call(
        functools.partial(far_kernel, step_size, n, ks),
        in_specs=[SMEM, VMEM, VMEM, VMEM],
        out_specs=[VMEM] * 2,
        out_shape=[
            jax.ShapeDtypeStruct((4, rows, width), jnp.float32),
            jax.ShapeDtypeStruct((2, 6, rows, width), jnp.float32),
        ],
        cost_estimate=costs(depth * rows * width),
        compiler_params=pltpu.CompilerParams(vmem_limit_bytes=20 * 1024 * 1024),
        name="march_far",
    )(mask, volume, density, border)


def finish_kernel(n, ks, sums, ends, near, far, *outs):
    rows, cols = near.shape
    strip = cols // n
    width = math.gcd(strip, 2 * LANES)
    me = lax.axis_index("depth")
    even = lax.rem(me, 2) == 0
    for j, k in enumerate(ks):
        at = target(n, me, k) * strip
        for c in range(strip // width):
            here = pl.ds(j * strip + c * width, width)
            planes = halves(
                even, near, far, pl.ds(pl.multiple_of(at + c * width, LANES), width)
            )
            colours = [sums[v, :, here] for v in range(3)]
            for end in range(2):
                g_depth = ends[end, 0, :, here] - planes[end]
                if end == 1:
                    g_depth = -g_depth
                shading = shade(g_depth, ends[end, 1, :, here], ends[end, 2, :, here])
                for v in range(3):
                    colours[v] = colours[v] + shading * ends[end, 3 + v, :, here]
            encode(outs[j], pl.ds(c * width, width), colours, sums[3, :, here])


def finish(sums, ends, near, far, n, ks):
    rows, cols = near.shape
    cells = rows * cols // n * len(ks)
    return pl.pallas_call(
        functools.partial(finish_kernel, n, ks),
        in_specs=[VMEM] * 4,
        out_specs=[VMEM] * len(ks),
        out_shape=[jax.ShapeDtypeStruct((4, rows, cols // n), jnp.int16)] * len(ks),
        cost_estimate=pl.CostEstimate(
            flops=60 * cells, bytes_accessed=64 * cells, transcendentals=4 * cells
        ),
        compiler_params=pltpu.CompilerParams(vmem_limit_bytes=16 * 1024 * 1024),
        name="finish",
    )(sums, ends, near, far)


def near_kernel(step_size, n, ks, mask, vol, density, border, near, far, *outs):
    depth, rows, cols = density.shape
    bricks = cols // LANES // n
    me = lax.axis_index("depth")
    even = lax.rem(me, 2) == 0
    for k, out in zip(ks, outs):
        at = target(n, me, k)

        def step(b, carry, at=at, out=out):
            place = at * bricks + b
            there = columns(b)
            keep = mask[0, place] != 0

            @pl.when(keep)
            def _():
                planes = halves(even, near, far, columns(place))

                def put(colours, optical):
                    encode(out, there, colours, optical)

                march_brick(
                    step_size, vol, density, border, mask, place, planes, None, put
                )

            @pl.when(jnp.logical_not(keep))
            def _():
                low = jnp.full((rows, LANES), -HALF, jnp.int32).astype(jnp.int16)
                for c in range(4):
                    out[c, :, there] = low

            return carry

        lax.fori_loop(0, bricks, step, 0)


def march_near(volume, density, border, near, far, mask, step_size, n, ks):
    channels, depth, rows, cols = volume.shape
    width = cols // n * len(ks)
    return pl.pallas_call(
        functools.partial(near_kernel, step_size, n, ks),
        in_specs=[SMEM] + [VMEM] * 5,
        out_specs=[VMEM] * len(ks),
        out_shape=[jax.ShapeDtypeStruct((4, rows, cols // n), jnp.int16)] * len(ks),
        cost_estimate=costs(depth * rows * width),
        compiler_params=pltpu.CompilerParams(vmem_limit_bytes=20 * 1024 * 1024),
        name="march_near",
    )(mask, volume, density, border, near, far)


def composite_kernel(ks, order, *refs):
    n = len(ks)
    parts, out = refs[:n], refs[n]
    me = lax.axis_index("depth")
    place = lax.broadcasted_iota(jnp.int32, order.shape, 1).astype(jnp.float32)
    slabs = order[...]
    rank = [
        jnp.sum(jnp.where(slabs == source(n, me, k), place, 0.0), axis=1, keepdims=True)
        for k in ks
    ]
    before = [[jnp.where(a < b, 1.0, 0.0) for a in rank] for b in rank]
    rows, strip = out.shape[1:]
    for b in range(strip // LANES):
        at = pl.ds(b * LANES, LANES)
        opacity = [
            eighth_power((part[3, :, at].astype(jnp.float32) + float(HALF)) * (1.0 / TOP))
            for part in parts
        ]
        whole = opacity[0]
        for k in range(1, n):
            whole = whole + opacity[k] * (1.0 - whole)
        picture = [None] * 3
        for k in range(n):
            share = opacity[k] * (1.0 / TOP)
            for e in range(n):
                if e != k:
                    share = share * (1.0 - before[k][e] * opacity[e])
            for c in range(3):
                term = share * (parts[k][c, :, at].astype(jnp.float32) + float(HALF))
                picture[c] = term if k == 0 else picture[c] + term
        for c in range(3):
            out[c, :, at] = picture[c]
        out[3, :, at] = whole


def composite(order, parts, ks):
    n = len(parts)
    rows, strip = parts[0].shape[1:]
    return pl.pallas_call(
        functools.partial(composite_kernel, ks),
        in_specs=[VMEM] * (n + 1),
        out_specs=VMEM,
        out_shape=jax.ShapeDtypeStruct((4, rows, strip), jnp.float32),
        compiler_params=pltpu.CompilerParams(vmem_limit_bytes=16 * 1024 * 1024),
        name="composite",
    )(order.reshape(1, n), *parts)


def on_device(volume, brick_mask, brick_order):
    channels, depth, rows, cols = volume.shape
    n = lax.axis_size("depth")
    assert lax.axis_size("tile") == 2
    step_size = 3.0 / (depth * n)
    mask = jnp.repeat(brick_mask, cols // brick_mask.shape[1] // LANES, axis=1)

    density, near, far, edge, mask = edges(volume, mask)
    border = lax.ppermute(edge, "tile", [(0, 1), (1, 0)])
    pairs = [(i, i ^ 1) for i in range(n) if i ^ 1 < n]
    near = lax.ppermute(near, "depth", pairs)
    pairs = [(i, i + 1) for i in range(1, n - 1, 2)]
    far = lax.ppermute(far, "depth", pairs + [(b, a) for a, b in pairs])

    first, second = [k ^ (n // 4) for k in rounds(n)[: n // 2]] + [0], rounds(n)[n // 2 : -1]
    sums, ends = march_far(volume, density, border, mask, step_size, n, first)
    strips = finish(sums, ends, near, far, n, first)
    strips, mask = lax.optimization_barrier((strips, mask))
    strips = list(strips) + list(
        march_near(volume, density, border, near, far, mask, step_size, n, second)
    )
    parts = [
        lax.ppermute(strip, "depth", partners(n, k)) if k else strip
        for strip, k in zip(strips, first + second)
    ]
    picture = composite(brick_order, parts, first + second)
    return lax.all_gather(picture, "tile", axis=1, tiled=True)


def solution(mesh):
    return jax.shard_map(
        on_device,
        mesh=mesh,
        in_specs=(
            P(None, ("parts", "depth"), "tile", None),
            P(("parts", "depth"), None),
            P("parts"),
        ),
        out_specs=P(None, "parts", "depth"),
        check_vma=False,
    )
```
